512 devices in a mesh: ctx: 64 (over z, y_lo, core), tp: 8 (over x, y_hi).
Axes of the slice: x: 4, y: 4 (y_hi: 2, y_lo: 2; y = y_hi * 2 + y_lo), z: 16, core: 2. Of those that a mesh axis runs over, the one named last changes fastest.
Arguments:
- byte_ids: int32 [32768], P('ctx'), may hold values from 0 to 255
- patch_lens: int32 [8192], P('ctx'), may hold values from 1 to 11, as said below
- byte_table: bfloat16 [256, 1024], replicated, may hold values from -6 to 6
- wq_cross: bfloat16 [1024, 2048], P(None, 'tp'), may hold values from -128 to 128
- wk_cross: bfloat16 [1024, 2048], P(None, 'tp'), may hold values from -1 to 1
- wv_cross: bfloat16 [1024, 2048], P(None, 'tp'), may hold values from -0.1875 to 0.1875
- norm_gain: float32 [2048], replicated, may hold values from 0.1 to 1.9
- wq_latent: bfloat16 [2048, 2048], P('ctx', 'tp'), may hold values from -8 to 8
- wk_latent: bfloat16 [2048, 2048], P('ctx', 'tp'), may hold values from -1 to 1
- wv_latent: bfloat16 [2048, 2048], P('ctx', 'tp'), may hold values from -0.125 to 0.125
Outputs:
- patch_latent: bfloat16 [8192, 2048], P('ctx', 'tp')
- latent_mixed: bfloat16 [8192, 2048], P('ctx', 'tp')
The draws below stay inside these ranges and needn't reach their ends.
Inputs may be any that keep to these rules, and one draw needn't show every extreme that they name: `patch_lens`: all patches together hold 32768 bytes; the patches of ctx index d begin at byte d * 512 + e_d with 0 <= e_d <= 256, e_0 = 0, and e_d = 256 for some d.
All inputs are finite; a program needn't handle non-finite values.
Results may differ from the reference program's by a relative error of at most 0.012.
The reference program's roundings to bfloat16 on the way count: a program that leaves them out, or rounds other values in their place, can miss the bound.
Values may be sent and summed in bfloat16 or wider, within the bound.
No kernel may reach another device: no remote copies, remote signals or barrier semaphores. Data moves between devices by JAX's collectives and lax.ppermute only.
A program may use at most 64 MiB of HBM per device.

```python
import math
import jax
import jax.numpy as jnp
import numpy as np
from jax import lax

DB = 1024
HD = 128
HEADS = 16
VOCAB = 256
LMAX = 11
P_DEV = 128
LAT = 2048
BYTES_DEV = 512
BYTES = 32768
PATCHES = 8192
N_CTX = 64


def draw_patch_lens(key, part):
    key = jax.random.fold_in(key, 11)
    key_drift, key_top, key_rank, key_noise = jax.random.split(key, 4)
    half_bytes = BYTES_DEV // 2
    drift = jax.random.randint(key_drift, (N_CTX + 1,), 0, half_bytes + 1)
    chosen = jax.random.randint(key_top, (), 1, N_CTX)
    places = jnp.arange(N_CTX + 1)
    drift = jnp.where(places == chosen - 1, 0, drift)
    drift = jnp.where(places == chosen, half_bytes, drift)
    drift = jnp.where((places == 0) | (places == N_CTX), 0, drift)
    totals = BYTES_DEV + drift[1:] - drift[:-1]
    extra = totals - P_DEV
    base = extra // P_DEV
    remain = extra - base * P_DEV
    ranks = jax.vmap(lambda sub_key: jax.random.permutation(sub_key, P_DEV))(jax.random.split(key_rank, N_CTX))
    extras = base[:, None] + (ranks < remain[:, None]).astype(jnp.int32)
    reach = jnp.minimum(base, 14 - base)[:, None]
    noise = jax.random.randint(key_noise, (N_CTX, P_DEV // 2), 0, 1 << 20) % (2 * reach + 1) - reach
    column = jnp.arange(P_DEV // 2)[None, :]
    noise = jnp.where(column == 0, reach, noise)
    lengths = 1 + extras + jnp.concatenate([noise, -noise], axis=1)
    return lengths.reshape(-1).astype(jnp.int32)


def clipped_normal(key, rows, cols, fan_in):
    return jnp.clip(jax.random.normal(key, (rows, cols), jnp.float32), -4.0, 4.0) * fan_in ** (-0.5)


def cross_base(key):
    key = jax.random.fold_in(key, 101)
    return clipped_normal(key, DB, LAT, DB)


def latent_base(key):
    key = jax.random.fold_in(key, 201)
    return clipped_normal(key, LAT, LAT, LAT)


def draw_wk_cross(key, part):
    shared = cross_base(key)
    return jnp.clip(shared, -1.0, 1.0).astype(jnp.bfloat16)


def draw_wq_cross(key, part):
    key = jax.random.fold_in(key, 102)
    key_noise = jax.random.fold_in(key, 0)
    noise = clipped_normal(key_noise, DB, LAT, DB)
    weight = noise
    return jnp.clip(weight, -128.0, 128.0).astype(jnp.bfloat16)


def draw_wk_latent(key, part):
    shared = latent_base(key)
    return jnp.clip(shared, -1.0, 1.0).astype(jnp.bfloat16)


def draw_wq_latent(key, part):
    key = jax.random.fold_in(key, 202)
    key_noise = jax.random.fold_in(key, 0)
    noise = 2.0 * clipped_normal(key_noise, LAT, LAT, LAT)
    weight = noise
    return jnp.clip(weight, -8.0, 8.0).astype(jnp.bfloat16)


def touch_ends(values, rng, smallest, largest):
    spot = [jax.random.randint(jax.random.fold_in(rng, axis), (), 0, length) for axis, length in enumerate(values.shape)]
    main_axis = values.shape.index(max(values.shape))
    next_to = spot[:main_axis] + [(spot[main_axis] + 1) % values.shape[main_axis]] + spot[main_axis + 1:]
    return values.at[tuple(spot)].set(smallest).at[tuple(next_to)].set(largest)


def block_levels(key, shape, pieces, smallest, top_value):
    def one(dim, shards_of):
        draws = jax.random.uniform(jax.random.fold_in(jax.random.fold_in(key, 6), dim), (shards_of,), jnp.float32, smallest / len(pieces), top_value / len(pieces))
        return jnp.repeat(jnp.exp(draws), shape[dim] // shards_of).reshape((-1,) + (1,) * (len(shape) - dim - 1))

    loudness = one(*pieces[0])
    for cut in pieces[1:]:
        loudness = loudness * one(*cut)
    return loudness


def rank_table(number_of, slope):
    loads = [(1 << 20) // math.isqrt(standing ** slope) + 1 for standing in range(1, number_of + 1)]
    scale = 1 + sum(loads) // (1 << 30)
    return np.cumsum(np.array([max(1, weight // scale) for weight in loads]))


def ranked(key, dims, number_of, slope):
    table = rank_table(number_of, slope)
    pick = jax.random.randint(jax.random.fold_in(key, 1), dims, 0, int(table[number_of - 1]))
    standing = jnp.searchsorted(jnp.asarray(table, jnp.int32), pick, side="right")
    return jax.random.permutation(jax.random.fold_in(key, 2), number_of)[standing].astype(jnp.int32)


def gaussian(key, dims, spread, most, cuts=(), kind=jnp.bfloat16):
    values = spread * jax.random.normal(key, dims, jnp.float32)
    if cuts:
        values = values * block_levels(key, dims, cuts, -0.22, 0.18)
    return jnp.clip(values, -most, most).astype(kind)


def setup_inputs(seed: int = 0) -> dict:
    arg_keys = jax.random.split(jax.random.key(seed), 11)
    byte_ids = touch_ends(ranked(arg_keys[0], (BYTES,), VOCAB, 2), jax.random.fold_in(arg_keys[0], 3), 0, VOCAB - 1).astype(jnp.int32)
    patch_lens = draw_patch_lens(jax.random.fold_in(arg_keys[10], 71), 0)
    byte_table = gaussian(arg_keys[2], (VOCAB, DB), 1.0, 6.0)
    wq_cross = draw_wq_cross(jax.random.fold_in(arg_keys[10], 71), 0)
    wk_cross = draw_wk_cross(jax.random.fold_in(arg_keys[10], 71), 0)
    wv_cross = gaussian(arg_keys[5], (DB, LAT), DB ** -0.5, 0.1875, ((1, 8),))
    norm_gain = jnp.clip(1.0 + 0.18 * jax.random.normal(arg_keys[6], (LAT,), jnp.float32), 0.1, 1.9)
    wq_latent = draw_wq_latent(jax.random.fold_in(arg_keys[10], 71), 0)
    wk_latent = draw_wk_latent(jax.random.fold_in(arg_keys[10], 71), 0)
    wv_latent = gaussian(arg_keys[9], (LAT, LAT), LAT ** -0.5, 0.125, ((0, 64), (1, 8)))
    return {"byte_ids": byte_ids, "patch_lens": patch_lens, "byte_table": byte_table, "wq_cross": wq_cross, "wk_cross": wk_cross, "wv_cross": wv_cross, "norm_gain": norm_gain, "wq_latent": wq_latent, "wk_latent": wk_latent, "wv_latent": wv_latent}


def reference(byte_ids, patch_lens, byte_table, wq_cross, wk_cross, wv_cross, norm_gain, wq_latent, wk_latent, wv_latent):
    scale = 1.0 / math.sqrt(HD)
    starts = (jnp.cumsum(patch_lens) - patch_lens).astype(jnp.int32)
    hidden = jnp.take(byte_table, byte_ids, axis=0)
    byte_q = jnp.dot(hidden, wq_cross, preferred_element_type=jnp.float32).astype(jnp.bfloat16)
    byte_k = jnp.dot(hidden, wk_cross, preferred_element_type=jnp.float32).astype(jnp.bfloat16)
    byte_v = jnp.dot(hidden, wv_cross, preferred_element_type=jnp.float32).astype(jnp.bfloat16)
    positions = jnp.arange(BYTES, dtype=jnp.int32)
    segment = (jnp.searchsorted(starts, positions, side='right') - 1).astype(jnp.int32)
    q_sums = jax.ops.segment_sum(byte_q.astype(jnp.float32), segment, num_segments=PATCHES)
    patch_q = (q_sums / patch_lens.astype(jnp.float32)[:, None]).astype(jnp.bfloat16)
    block = math.gcd(PATCHES, 512)

    def cross_block(block_pos):
        first = (block_pos * block).astype(jnp.int32)
        start_rows = lax.dynamic_slice_in_dim(starts, first, block)
        len_rows = lax.dynamic_slice_in_dim(patch_lens, first, block)
        query = lax.dynamic_slice_in_dim(patch_q, first, block).astype(jnp.float32).reshape(block, HEADS, HD)
        offsets = jnp.arange(LMAX, dtype=jnp.int32)
        index_grid = jnp.minimum(start_rows[:, None] + offsets[None, :], BYTES - 1).astype(jnp.int32)
        keys = jnp.take(byte_k, index_grid, axis=0).astype(jnp.float32).reshape(block, LMAX, HEADS, HD)
        values = jnp.take(byte_v, index_grid, axis=0).astype(jnp.float32).reshape(block, LMAX, HEADS, HD)
        scores = jnp.einsum('phd,pjhd->hpj', query, keys) * scale
        valid = offsets[None, :] < len_rows[:, None]
        scores = jnp.where(valid[None], scores, jnp.float32(-1e+30))
        top = lax.optimization_barrier(jnp.max(scores, axis=-1, keepdims=True))
        expo = jnp.exp(scores - top) * valid[None].astype(jnp.float32)
        weights = (expo / lax.optimization_barrier(jnp.sum(expo, axis=-1, keepdims=True))).astype(jnp.bfloat16)
        weights = lax.optimization_barrier(weights).astype(jnp.float32)
        result = jnp.einsum('hpj,pjhd->phd', weights, values)
        return result.reshape(block, LAT).astype(jnp.bfloat16)
    patch_latent = lax.map(cross_block, jnp.arange(PATCHES // block, dtype=jnp.int32)).reshape(PATCHES, LAT)
    latent32 = patch_latent.astype(jnp.float32)
    inverse = lax.rsqrt(lax.optimization_barrier(jnp.mean(latent32 * latent32, axis=-1, keepdims=True)) + 1e-05)
    normed = (latent32 * inverse * norm_gain[None, :]).astype(jnp.bfloat16)
    lat_q = jnp.dot(normed, wq_latent, preferred_element_type=jnp.float32).astype(jnp.bfloat16)
    lat_k = jnp.dot(normed, wk_latent, preferred_element_type=jnp.float32).astype(jnp.bfloat16)
    lat_v = jnp.dot(normed, wv_latent, preferred_element_type=jnp.float32).astype(jnp.bfloat16)
    keys_all = lat_k.astype(jnp.float32).reshape(PATCHES, HEADS, HD)
    values_all = lat_v.astype(jnp.float32).reshape(PATCHES, HEADS, HD)
    qblock = math.gcd(PATCHES, 256)
    key_index = jnp.arange(PATCHES, dtype=jnp.int32)

    def latent_block(block_pos):
        first = (block_pos * qblock).astype(jnp.int32)
        query = lax.dynamic_slice_in_dim(lat_q, first, qblock).astype(jnp.float32).reshape(qblock, HEADS, HD)
        query_index = first + jnp.arange(qblock, dtype=jnp.int32)
        allowed = key_index[None, :] <= query_index[:, None]
        scores = jnp.einsum('qhd,khd->hqk', query, keys_all) * scale
        scores = jnp.where(allowed[None], scores, jnp.float32(-1e+30))
        top = lax.optimization_barrier(jnp.max(scores, axis=-1, keepdims=True))
        expo = jnp.exp(scores - top) * allowed[None].astype(jnp.float32)
        total = lax.optimization_barrier(jnp.sum(expo, axis=-1, keepdims=True))
        weights = lax.optimization_barrier(expo.astype(jnp.bfloat16)).astype(jnp.float32)
        result = jnp.einsum('hqk,khd->qhd', weights, values_all) / jnp.transpose(total, (1, 0, 2))
        return result.reshape(qblock, LAT).astype(jnp.bfloat16)
    latent_mixed = lax.map(latent_block, jnp.arange(PATCHES // qblock, dtype=jnp.int32)).reshape(PATCHES, LAT)
    return (patch_latent, latent_mixed)
```

```python
import math

import jax
import jax.numpy as jnp
from jax import lax
from jax.experimental import pallas as pl
from jax.experimental.pallas import tpu as pltpu
from jax.sharding import Mesh
from jax.sharding import PartitionSpec as P

HD = 128
SCALE = 1.0 / math.sqrt(HD)
NEG = -1e30
N_CTX = 64
N_TP = 8
BYTES_DEV = 512
P_DEV = 128
W_ROWS = 32
ROWS = 3 * W_ROWS
MSG = ROWS + 16
VMEM = 56 * 1024 * 1024

CTX = ("z", "yl", "c")
TP = ("x", "yh")
PLANE = ("yl", "x", "yh")
TURN = ("z", "x", "yh")


def turns():
    same, other = [], []
    for z in range(16):
        for t in range(N_TP):
            same.append((z * N_TP + t, (2 * t + z % 2) * N_TP + z // 2))
            other.append((z * N_TP + t, (2 * t + 1 - z % 2) * N_TP + z // 2))
    return same, other


def back(pairs):
    return [(target, source) for source, target in pairs]


def to_all(value, axes, count):
    return lax.all_to_all(jnp.broadcast_to(value[None], (count, *value.shape)), axes, 0, 0)


def nt_dot(a, b):
    return lax.dot_general(a, b, (((1,), (1,)), ((), ())), preferred_element_type=jnp.float32)


def lens_before(d, c, own_ref, other_ref):
    total = jnp.zeros((), jnp.float32)
    for ref, core in ((own_ref, c), (other_ref, 1 - c)):
        tiles = ref[:, :, ROWS:MSG, :].astype(jnp.float32)
        unit, b, row = (lax.broadcasted_iota(jnp.int32, tiles.shape, i) for i in range(3))
        place = 8 * (unit % 8) + 4 * b + 2 * (unit // 8) + core
        total = total + jnp.sum(jnp.where((row == 4) & (place < d), tiles, 0.0))
    return total


def byte_counts(d, c, own_ref, other_ref):
    follow = jnp.where(d < N_CTX - 1, d + 1, d - 1)

    def tile(ref, place):
        unit = ((place // 2) % 2) * 8 + place // 8
        return ref[unit, (place // 4) % 2, ROWS:MSG, :].astype(jnp.float32)

    here, beyond = tile(own_ref, d), tile(other_ref, follow)
    begin = lens_before(d, c, own_ref, other_ref) - (d * BYTES_DEV).astype(jnp.float32)
    lens_row = here[4:5, :]
    row = lax.broadcasted_iota(jnp.int32, (P_DEV, P_DEV), 0)
    col = lax.broadcasted_iota(jnp.int32, (P_DEV, P_DEV), 1)
    lens = jnp.sum(jnp.where(col == row, lens_row, 0.0), axis=1, keepdims=True)
    start = begin + jnp.sum(jnp.where(col < row, lens_row, 0.0), axis=1, keepdims=True)
    end = start + lens
    value = (lax.broadcasted_iota(jnp.int32, (256, P_DEV), 0) + 128 * c) % 256
    value = value.astype(jnp.float32)
    slot = col.astype(jnp.float32)
    counts = jnp.zeros((P_DEV, 256), jnp.float32)
    for chunk in range(6):
        ids = here[chunk : chunk + 1, :] if chunk < 4 else beyond[chunk - 4 : chunk - 3, :]
        at = slot + 128.0 * chunk
        member = ((at >= start) & (at < end)).astype(jnp.bfloat16)
        onehot = (value == ids).astype(jnp.bfloat16)
        counts = counts + nt_dot(member, onehot)
    return counts, lens


def two_heads(counts, lens, table):
    pooled = jnp.dot(counts.astype(jnp.bfloat16), table[:, :256], preferred_element_type=jnp.float32)
    query = (pooled / lens).astype(jnp.bfloat16)
    outs = []
    for a in range(2):
        lanes = slice(a * HD, (a + 1) * HD)
        scores = nt_dot(query[:, lanes], table[:, 256 + a * HD : 256 + (a + 1) * HD]) * SCALE
        scores = jnp.where(counts > 0.0, scores, NEG)
        expo = jnp.exp(scores - jnp.max(scores, axis=-1, keepdims=True))
        norm = jnp.sum(expo * counts, axis=-1, keepdims=True)
        weights = (expo * (1.0 / norm)).astype(jnp.bfloat16).astype(jnp.float32) * counts
        high = weights.astype(jnp.bfloat16)
        low = (weights - high.astype(jnp.float32)).astype(jnp.bfloat16)
        vals = table[:, 512 + a * HD : 512 + (a + 1) * HD]
        out = jnp.dot(high, vals, preferred_element_type=jnp.float32)
        out = out + jnp.dot(low, vals, preferred_element_type=jnp.float32)
        outs.append(out.astype(jnp.bfloat16))
    return jnp.concatenate(outs, axis=1)


def encode_kernel(
    place_ref, tab_own, tab_other, msg_own, msg_other, gain_ref, q_ref, kv_ref, latent, weight
):
    c, yl, t = place_ref[0], place_ref[1], place_ref[2]
    parts = [byte_counts(8 * t + 4 * b + 2 * yl + c, c, msg_own, msg_other) for b in range(2)]
    counts = jnp.concatenate([part[0] for part in parts], axis=0)
    lens = jnp.concatenate([part[1] for part in parts], axis=0)

    def heads(tt, squares):
        table = jnp.concatenate([tab_own[tt], tab_other[tt]], axis=0)
        out = two_heads(counts, lens, table)
        latent[tt] = out
        wide = out.astype(jnp.float32)
        for ref, core in ((msg_own, c), (msg_other, 1 - c)):
            for b in range(2):
                for side in range(2):
                    first = pl.multiple_of(W_ROWS * (4 * b + 2 * side + core), W_ROWS)
                    for n in range(3):
                        weight[tt, pl.ds(first, W_ROWS), n * HD : (n + 1) * HD] = ref[
                            8 * side + tt, b, n * W_ROWS : (n + 1) * W_ROWS, :
                        ]
        return squares + jnp.sum(wide * wide, axis=-1, keepdims=True)

    squares = lax.fori_loop(0, N_TP, heads, jnp.zeros((2 * P_DEV, 1), jnp.float32))
    inverse = lax.rsqrt(squares / 2048.0 + 1e-05)
    total = jnp.zeros((2 * P_DEV, 3 * HD), jnp.float32)
    for tt in range(N_TP):
        normed = latent[tt].astype(jnp.float32) * inverse * gain_ref[tt : tt + 1, :]
        total = total + jnp.dot(
            normed.astype(jnp.bfloat16), weight[tt], preferred_element_type=jnp.float32
        )
    total = total.astype(jnp.bfloat16)
    q_ref[...] = total[:, :HD]
    kv_ref[...] = total[:, HD:]


def latent_kernel(place_ref, tab_own, tab_other, msg_own, msg_other, out_ref):
    c, t, d = place_ref[0], place_ref[2], place_ref[3]
    counts, lens = byte_counts(d, c, msg_own, msg_other)
    table = jnp.concatenate([tab_own[t], tab_other[t]], axis=0)
    out_ref[...] = two_heads(counts, lens, table)


def attend_kernel(place_ref, q_ref, kv_own, kv_other, out_ref, scores):
    c, yl, t = place_ref[0], place_ref[1], place_ref[2]
    query = q_ref[...]
    size = 2 * P_DEV
    row = lax.broadcasted_iota(jnp.int32, (size, size), 0)
    col = lax.broadcasted_iota(jnp.int32, (size, size), 1)
    row_at = 1024 * t + 512 * (row // P_DEV) + 256 * yl + P_DEV * c + row % P_DEV
    col_at = 512 * (col // P_DEV) + col % P_DEV

    def first(tt, top):
        for i, (ref, core) in enumerate(((kv_own, c), (kv_other, 1 - c))):
            for side in range(2):
                s = nt_dot(query, ref[8 * side + tt, :, :HD]) * SCALE
                s = jnp.where(col_at + (1024 * tt + 256 * side + P_DEV * core) <= row_at, s, NEG)
                scores[tt, 2 * i + side] = s
                top = jnp.maximum(top, jnp.maximum(s[:, :HD], s[:, HD:]))
        return top

    top = lax.fori_loop(0, t + 1, first, jnp.full((size, HD), NEG, jnp.float32))
    top = jnp.max(top, axis=-1, keepdims=True)

    def second(tt, carry):
        norm, acc = carry
        for i, ref in enumerate((kv_own, kv_other)):
            for side in range(2):
                e = jnp.exp(scores[tt, 2 * i + side] - top)
                norm = norm + (e[:, :HD] + e[:, HD:])
                acc = acc + jnp.dot(
                    e.astype(jnp.bfloat16),
                    ref[8 * side + tt, :, HD:],
                    preferred_element_type=jnp.float32,
                )
        return norm, acc

    zero = jnp.zeros((size, HD), jnp.float32)
    norm, acc = lax.fori_loop(0, t + 1, second, (zero, zero))
    out = acc / jnp.sum(norm, axis=-1, keepdims=True)
    out_ref[...] = out.astype(jnp.bfloat16)


def call(body, outs, scratch, flops, *args):
    vmem = pl.BlockSpec(memory_space=pltpu.VMEM)
    smem = pl.BlockSpec(memory_space=pltpu.SMEM)
    return pl.pallas_call(
        body,
        out_shape=[jax.ShapeDtypeStruct(shape, jnp.bfloat16) for shape in outs],
        in_specs=[smem] + [vmem] * (len(args) - 1),
        out_specs=[vmem] * len(outs),
        scratch_shapes=scratch,
        compiler_params=pltpu.CompilerParams(vmem_limit_bytes=VMEM),
        cost_estimate=pl.CostEstimate(flops=flops, bytes_accessed=4 << 20, transcendentals=1 << 20),
    )(*args)


def on_device(
    byte_ids,
    patch_lens,
    byte_table,
    wq_cross,
    wk_cross,
    wv_cross,
    norm_gain,
    wq_latent,
    wk_latent,
    wv_latent,
):
    z, yl, c = (lax.axis_index(name) for name in CTX)
    t = lax.axis_index("x") * 2 + lax.axis_index("yh")
    place = jnp.stack([c, yl, t, 4 * z + 2 * yl + c]).astype(jnp.int32)
    swap = [(0, 1), (1, 0)]
    same, other = turns()

    ints = jnp.concatenate([byte_ids, patch_lens]).astype(jnp.bfloat16).reshape(5, HD)
    ints = jnp.pad(ints, ((0, 11), (0, 0)))
    latent = (wq_latent, wk_latent, wv_latent)
    messages = [
        jnp.concatenate([w[:, a * HD : (a + 1) * HD] for w in latent] + [ints], axis=0) for a in range(2)
    ]
    odd = z % 2 == 1
    got_same = lax.ppermute(jnp.where(odd, messages[1], messages[0]), TURN, same)
    got_other = lax.ppermute(jnp.where(odd, messages[0], messages[1]), TURN, other)
    message = jnp.stack(
        [jnp.where(odd, got_other, got_same), jnp.where(odd, got_same, got_other)]
    )

    rows = lax.dynamic_slice_in_dim(byte_table, 128 * c, 128, axis=0)
    tables = jnp.concatenate(
        [
            jnp.dot(rows, w, preferred_element_type=jnp.float32).astype(jnp.bfloat16)
            for w in (wq_cross, wk_cross, wv_cross)
        ],
        axis=1,
    )
    tab_own = to_all(tables, TP, N_TP)
    tab_other = lax.ppermute(tab_own, "c", swap)
    msg_own = to_all(message, PLANE, 16)
    msg_other = lax.ppermute(msg_own, "c", swap)

    q, kv = call(
        encode_kernel,
        [(2 * P_DEV, HD), (2 * P_DEV, 2 * HD)],
        [pltpu.VMEM((N_TP, 256, 256), jnp.bfloat16), pltpu.VMEM((N_TP, 256, 3 * HD), jnp.bfloat16)],
        1 << 30,
        place,
        tab_own,
        tab_other,
        msg_own,
        msg_other,
        norm_gain.reshape(N_TP, 256),
    )
    kv_own = to_all(kv, PLANE, 16)
    kv_other = lax.ppermute(kv_own, "c", swap)
    (mixed,) = call(
        attend_kernel,
        [(2 * P_DEV, HD)],
        [pltpu.VMEM((N_TP, 4, 2 * P_DEV, 2 * P_DEV), jnp.float32)],
        1 << 30,
        place,
        q,
        kv_own,
        kv_other,
    )
    sent_same = jnp.where(odd, mixed[P_DEV:], mixed[:P_DEV])
    sent_other = jnp.where(odd, mixed[:P_DEV], mixed[P_DEV:])
    head_same = lax.ppermute(sent_same, TURN, back(same))
    head_other = lax.ppermute(sent_other, TURN, back(other))
    (patch_latent,) = call(
        latent_kernel, [(P_DEV, 256)], [], 1 << 26, place, tab_own, tab_other, msg_own, msg_other
    )
    latent_mixed = jnp.concatenate(
        [jnp.where(odd, head_other, head_same), jnp.where(odd, head_same, head_other)], axis=1
    )
    return (patch_latent, latent_mixed)


def solution(mesh):
    fine = Mesh(mesh.devices.reshape(16, 2, 2, 4, 2), ("z", "yl", "c", "x", "yh"))
    return jax.shard_map(
        on_device,
        mesh=fine,
        in_specs=(
            P(CTX),
            P(CTX),
            P(),
            P(None, TP),
            P(None, TP),
            P(None, TP),
            P(),
            P(CTX, TP),
            P(CTX, TP),
            P(CTX, TP),
        ),
        out_specs=(P(CTX, TP), P(CTX, TP)),
        check_vma=False,
    )
```

```python
import math

import jax
import jax.numpy as jnp
from jax import lax
from jax.experimental import pallas as pl
from jax.experimental.pallas import tpu as pltpu
from jax.sharding import Mesh
from jax.sharding import PartitionSpec as P

HD = 128
SCALE = 1.0 / math.sqrt(HD)
NEG = -1e30
N_CTX = 64
N_TP = 8
BYTES_DEV = 512
P_DEV = 128
W_ROWS = 32
VALUES = 64
TABLE = 6 * VALUES
ROWS = TABLE + 2 * 3 * W_ROWS
MSG = ROWS + 2 * 16
VMEM = 56 * 1024 * 1024

CTX = ("z", "yl", "c")
TP = ("x", "yh")
PLANE = ("x", "yh", "yl")
TURN = ("z", "x", "yh")


def turns():
    same, other = [], []
    for z in range(16):
        for t in range(N_TP):
            far, low = z // 8, min(z, 15 - z)
            same.append((z * N_TP + t, (2 * t + far) * N_TP + low))
            other.append((z * N_TP + t, (2 * t + 1 - far) * N_TP + low))
    return same, other


def back(pairs):
    return [(target, source) for source, target in pairs]


def to_all(value, axes, count):
    return lax.all_to_all(jnp.broadcast_to(value[None], (count, *value.shape)), axes, 0, 0)


def nt_dot(a, b):
    return lax.dot_general(a, b, (((1,), (1,)), ((), ())), preferred_element_type=jnp.float32)


def lens_before(d, c, own_ref, other_ref):
    total = jnp.zeros((), jnp.float32)
    for ref, core in ((own_ref, c), (other_ref, 1 - c)):
        for b in range(2):
            tiles = ref[:, ROWS + 16 * b : ROWS + 16 * (b + 1), :].astype(jnp.float32)
            unit, row = (lax.broadcasted_iota(jnp.int32, tiles.shape, i) for i in range(2))
            z = unit // 2 if b == 0 else 15 - unit // 2
            place = 4 * z + 2 * (unit % 2) + core
            total = total + jnp.sum(jnp.where((row == 4) & (place < d), tiles, 0.0))
    return total


def byte_counts(d, c, own_ref, other_ref):
    follow = jnp.where(d < N_CTX - 1, d + 1, d - 1)

    def tile(ref, place):
        z = place // 4
        unit = 2 * jnp.minimum(z, 15 - z) + (place // 2) % 2
        first = pl.multiple_of(ROWS + 16 * (z // 8), 16)
        return ref[unit, pl.ds(first, 16), :].astype(jnp.float32)

    here, beyond = tile(own_ref, d), tile(other_ref, follow)
    begin = lens_before(d, c, own_ref, other_ref) - (d * BYTES_DEV).astype(jnp.float32)
    lens_row = here[4:5, :]
    row = lax.broadcasted_iota(jnp.int32, (P_DEV, P_DEV), 0)
    col = lax.broadcasted_iota(jnp.int32, (P_DEV, P_DEV), 1)
    lens = jnp.sum(jnp.where(col == row, lens_row, 0.0), axis=1, keepdims=True)
    start = begin + jnp.sum(jnp.where(col < row, lens_row, 0.0), axis=1, keepdims=True)
    end = start + lens
    value = (lax.broadcasted_iota(jnp.int32, (256, P_DEV), 0) + 128 * c) % 256
    value = value.astype(jnp.float32)
    slot = col.astype(jnp.float32)
    counts = jnp.zeros((P_DEV, 256), jnp.float32)
    for chunk in range(6):
        ids = here[chunk : chunk + 1, :] if chunk < 4 else beyond[chunk - 4 : chunk - 3, :]
        at = slot + 128.0 * chunk
        member = ((at >= start) & (at < end)).astype(jnp.bfloat16)
        onehot = (value == ids).astype(jnp.bfloat16)
        counts = counts + nt_dot(member, onehot)
    return counts, lens


def table_of(tt, own_ref, other_ref):
    def piece(i):
        rows = slice(i * VALUES, (i + 1) * VALUES)
        parts = [ref[2 * tt + side, rows, :] for ref in (own_ref, other_ref) for side in range(2)]
        return jnp.concatenate(parts, axis=0)

    return [piece(i) for i in range(6)]


def two_heads(counts, lens, table):
    times = counts.astype(jnp.bfloat16)
    share = 1.0 / lens
    hide = jnp.where(counts > 0.0, 0.0, NEG)
    outs = []
    for a in range(2):
        queries, keys, values = table[a], table[2 + a], table[4 + a]
        pooled = jnp.dot(times, queries, preferred_element_type=jnp.float32)
        scores = nt_dot((pooled * share).astype(jnp.bfloat16), keys) * SCALE + hide
        expo = jnp.exp(scores - jnp.max(scores, axis=-1, keepdims=True))
        norm = jnp.sum(expo * counts, axis=-1, keepdims=True)
        weights = (expo * (1.0 / norm)).astype(jnp.bfloat16).astype(jnp.float32) * counts
        out = jnp.dot(weights.astype(jnp.bfloat16), values, preferred_element_type=jnp.float32)
        outs.append(out.astype(jnp.bfloat16))
    return jnp.concatenate(outs, axis=1)


def encode_kernel(place_ref, own_ref, other_ref, gain_ref, q_ref, kv_ref, latent, weight):
    c, yl, t = place_ref[0], place_ref[1], place_ref[2]
    parts = [
        byte_counts(4 * z + 2 * yl + c, c, own_ref, other_ref) for z in (t, 2 * N_TP - 1 - t)
    ]
    counts = jnp.concatenate([part[0] for part in parts], axis=0)
    lens = jnp.concatenate([part[1] for part in parts], axis=0)

    def heads(tt, squares):
        out = two_heads(counts, lens, table_of(tt, own_ref, other_ref))
        latent[tt] = out
        wide = out.astype(jnp.float32)
        for ref, core in ((own_ref, c), (other_ref, 1 - c)):
            for b in range(2):
                z = tt if b == 0 else 15 - tt
                for side in range(2):
                    first = pl.multiple_of(W_ROWS * (4 * (z % 2) + 2 * side + core), W_ROWS)
                    for n in range(3):
                        start = TABLE + (3 * b + n) * W_ROWS
                        weight[z // 2, pl.ds(first, W_ROWS), n * HD : (n + 1) * HD] = ref[
                            2 * tt + side, start : start + W_ROWS, :
                        ]
        return squares + jnp.sum(wide * wide, axis=-1, keepdims=True)

    squares = lax.fori_loop(0, N_TP, heads, jnp.zeros((2 * P_DEV, 1), jnp.float32))
    inverse = lax.rsqrt(squares / 2048.0 + 1e-05)
    total = jnp.zeros((2 * P_DEV, 3 * HD), jnp.float32)
    for tt in range(N_TP):
        normed = latent[tt].astype(jnp.float32) * inverse * gain_ref[tt : tt + 1, :]
        total = total + jnp.dot(
            normed.astype(jnp.bfloat16), weight[tt], preferred_element_type=jnp.float32
        )
    total = total.astype(jnp.bfloat16)
    q_ref[...] = total[:, :HD]
    kv_ref[...] = total[:, HD:]


def latent_kernel(place_ref, own_ref, other_ref, out_ref):
    c, t, d = place_ref[0], place_ref[2], place_ref[3]
    counts, lens = byte_counts(d, c, own_ref, other_ref)
    out_ref[...] = two_heads(counts, lens, table_of(t, own_ref, other_ref))


def table_kernel(place_ref, table_ref, wq_ref, wk_ref, wv_ref, out_ref):
    first = 2 * VALUES * place_ref[0] + VALUES * place_ref[1]
    rows = table_ref[pl.ds(pl.multiple_of(first, VALUES), VALUES), :]
    for i, ref in enumerate((wq_ref, wk_ref, wv_ref)):
        part = jnp.dot(rows, ref[...], preferred_element_type=jnp.float32).astype(jnp.bfloat16)
        for a in range(2):
            start = (2 * i + a) * VALUES
            out_ref[start : start + VALUES, :] = part[:, a * HD : (a + 1) * HD]


def attend_kernel(place_ref, q_ref, kv_own, kv_other, out_ref, scores):
    c, yl, t = place_ref[0], place_ref[1], place_ref[2]
    query = q_ref[...]
    size = 2 * P_DEV
    row = lax.broadcasted_iota(jnp.int32, (size, size), 0)
    col = lax.broadcasted_iota(jnp.int32, (size, size), 1)
    last = 2 * N_TP - 1

    def places(index, tt):
        z = jnp.where(index < P_DEV, tt, last - tt)
        return 512 * z + index % P_DEV

    row_at = places(row, t) + 256 * yl + P_DEV * c

    def first(tt, top):
        for i, (ref, core) in enumerate(((kv_own, c), (kv_other, 1 - c))):
            for side in range(2):
                s = nt_dot(query, ref[2 * tt + side, :, :HD]) * SCALE
                s = jnp.where(places(col, tt) + (256 * side + P_DEV * core) <= row_at, s, NEG)
                scores[tt, 2 * i + side] = s
                top = jnp.maximum(top, jnp.maximum(s[:, :HD], s[:, HD:]))
        return top

    top = lax.fori_loop(0, N_TP, first, jnp.full((size, HD), NEG, jnp.float32))
    top = jnp.max(top, axis=-1, keepdims=True)

    def second(tt, carry):
        norm, acc = carry
        for i, ref in enumerate((kv_own, kv_other)):
            for side in range(2):
                e = jnp.exp(scores[tt, 2 * i + side] - top)
                norm = norm + (e[:, :HD] + e[:, HD:])
                acc = acc + jnp.dot(
                    e.astype(jnp.bfloat16),
                    ref[2 * tt + side, :, HD:],
                    preferred_element_type=jnp.float32,
                )
        return norm, acc

    zero = jnp.zeros((size, HD), jnp.float32)
    norm, acc = lax.fori_loop(0, N_TP, second, (zero, zero))
    out = acc / jnp.sum(norm, axis=-1, keepdims=True)
    out_ref[...] = out.astype(jnp.bfloat16)


def call(body, outs, scratch, flops, *args):
    vmem = pl.BlockSpec(memory_space=pltpu.VMEM)
    smem = pl.BlockSpec(memory_space=pltpu.SMEM)
    return pl.pallas_call(
        body,
        out_shape=[jax.ShapeDtypeStruct(shape, jnp.bfloat16) for shape in outs],
        in_specs=[smem] + [vmem] * (len(args) - 1),
        out_specs=[vmem] * len(outs),
        scratch_shapes=scratch,
        compiler_params=pltpu.CompilerParams(vmem_limit_bytes=VMEM),
        cost_estimate=pl.CostEstimate(flops=flops, bytes_accessed=4 << 20, transcendentals=1 << 20),
    )(*args)


def run_table(*args):
    return call(table_kernel, [(TABLE, HD)], [], 1 << 28, *args)[0]


def run_encode(*args):
    return call(
        encode_kernel,
        [(2 * P_DEV, HD), (2 * P_DEV, 2 * HD)],
        [pltpu.VMEM((N_TP, 256, 256), jnp.bfloat16), pltpu.VMEM((N_TP, 256, 3 * HD), jnp.bfloat16)],
        1 << 30,
        *args,
    )


def run_latent(*args):
    return call(latent_kernel, [(P_DEV, 256)], [], 1 << 26, *args)[0]


def run_attend(*args):
    scratch = [pltpu.VMEM((N_TP, 4, 2 * P_DEV, 2 * P_DEV), jnp.float32)]
    return call(attend_kernel, [(2 * P_DEV, HD)], scratch, 1 << 30, *args)[0]


def on_device(
    byte_ids,
    patch_lens,
    byte_table,
    wq_cross,
    wk_cross,
    wv_cross,
    norm_gain,
    wq_latent,
    wk_latent,
    wv_latent,
):
    z, yl, c = (lax.axis_index(name) for name in CTX)
    t = lax.axis_index("x") * 2 + lax.axis_index("yh")
    place = jnp.stack([c, yl, t, 4 * z + 2 * yl + c]).astype(jnp.int32)
    swap = [(0, 1), (1, 0)]
    same, other = turns()

    ints = jnp.concatenate([byte_ids, patch_lens]).astype(jnp.bfloat16).reshape(5, HD)
    ints = jnp.pad(ints, ((0, 11), (0, 0)))
    latent = (wq_latent, wk_latent, wv_latent)
    messages = [
        jnp.concatenate([w[:, a * HD : (a + 1) * HD] for w in latent] + [ints], axis=0) for a in range(2)
    ]
    far, odd = z >= 8, z % 2 == 1
    got_same = lax.ppermute(jnp.where(far, messages[1], messages[0]), TURN, same)
    got_other = lax.ppermute(jnp.where(far, messages[0], messages[1]), TURN, other)

    table = run_table(place, byte_table, wq_cross, wk_cross, wv_cross)
    table, got_same, got_other = lax.optimization_barrier((table, got_same, got_other))
    near = jnp.where(odd, got_other, got_same)
    away = jnp.where(odd, got_same, got_other)
    cut = 3 * W_ROWS
    message = jnp.concatenate([table, near[:cut], away[:cut], near[cut:], away[cut:]], axis=0)
    own = to_all(message, PLANE, 16)
    other_core = lax.ppermute(own, "c", swap)

    gain = norm_gain.reshape(N_TP, 256)
    q, kv = run_encode(place, own, other_core, gain)
    kv_own = to_all(kv, PLANE, 16)
    kv_other = lax.ppermute(kv_own, "c", swap)
    mixed = run_attend(place, q, kv_own, kv_other)
    sent_same = jnp.where(odd, mixed[P_DEV:], mixed[:P_DEV])
    sent_other = jnp.where(odd, mixed[:P_DEV], mixed[P_DEV:])
    head_same = lax.ppermute(sent_same, TURN, back(same))
    head_other = lax.ppermute(sent_other, TURN, back(other))
    patch_latent = run_latent(place, own, other_core)
    latent_mixed = jnp.concatenate(
        [jnp.where(far, head_other, head_same), jnp.where(far, head_same, head_other)], axis=1
    )
    return (patch_latent, latent_mixed)


def solution(mesh):
    fine = Mesh(mesh.devices.reshape(16, 2, 2, 4, 2), ("z", "yl", "c", "x", "yh"))
    return jax.shard_map(
        on_device,
        mesh=fine,
        in_specs=(
            P(CTX),
            P(CTX),
            P(),
            P(None, TP),
            P(None, TP),
            P(None, TP),
            P(),
            P(CTX, TP),
            P(CTX, TP),
            P(CTX, TP),
        ),
        out_specs=(P(CTX, TP), P(CTX, TP)),
        check_vma=False,
    )
```

```python
import math

import jax
import jax.numpy as jnp
from jax import lax
from jax.experimental import pallas as pl
from jax.experimental.pallas import tpu as pltpu
from jax.sharding import Mesh
from jax.sharding import PartitionSpec as P

HD = 128
SCALE = 1.0 / math.sqrt(HD)
NEG = -1e30
N_CTX = 64
N_TP = 8
BYTES_DEV = 512
P_DEV = 128
W_ROWS = 32
VALUES = 128
ROWS = 2 * 3 * W_ROWS
MSG = ROWS + 2 * 16
PART = 2 * P_DEV + 8
VMEM = 56 * 1024 * 1024

CTX = ("z", "yl", "c")
TP = ("x", "yh")
PLANE = ("x", "yh", "yl")
TURN = ("z", "x", "yh")


def turns():
    same, other = [], []
    for z in range(16):
        for t in range(N_TP):
            far, low = z // 8, min(z, 15 - z)
            same.append((z * N_TP + t, (2 * t + far) * N_TP + low))
            other.append((z * N_TP + t, (2 * t + 1 - far) * N_TP + low))
    return same, other


def back(pairs):
    return [(target, source) for source, target in pairs]


def to_all(value, axes, count):
    return lax.all_to_all(jnp.broadcast_to(value[None], (count, *value.shape)), axes, 0, 0)


def nt_dot(a, b):
    return lax.dot_general(a, b, (((1,), (1,)), ((), ())), preferred_element_type=jnp.float32)


def lens_before(d, c, own_ref, other_ref):
    total = jnp.zeros((), jnp.float32)
    for ref, core in ((own_ref, c), (other_ref, 1 - c)):
        for b in range(2):
            tiles = ref[:, ROWS + 16 * b : ROWS + 16 * (b + 1), :].astype(jnp.float32)
            unit, row = (lax.broadcasted_iota(jnp.int32, tiles.shape, i) for i in range(2))
            z = unit // 2 if b == 0 else 15 - unit // 2
            place = 4 * z + 2 * (unit % 2) + core
            total = total + jnp.sum(jnp.where((row == 4) & (place < d), tiles, 0.0))
    return total


def byte_counts(d, c, own_ref, other_ref):
    follow = jnp.where(d < N_CTX - 1, d + 1, d - 1)

    def tile(ref, place):
        z = place // 4
        unit = 2 * jnp.minimum(z, 15 - z) + (place // 2) % 2
        first = pl.multiple_of(ROWS + 16 * (z // 8), 16)
        return ref[unit, pl.ds(first, 16), :].astype(jnp.float32)

    here, beyond = tile(own_ref, d), tile(other_ref, follow)
    begin = lens_before(d, c, own_ref, other_ref) - (d * BYTES_DEV).astype(jnp.float32)
    lens_row = here[4:5, :]
    row = lax.broadcasted_iota(jnp.int32, (P_DEV, P_DEV), 0)
    col = lax.broadcasted_iota(jnp.int32, (P_DEV, P_DEV), 1)
    lens = jnp.sum(jnp.where(col == row, lens_row, 0.0), axis=1, keepdims=True)
    start = begin + jnp.sum(jnp.where(col < row, lens_row, 0.0), axis=1, keepdims=True)
    end = start + lens
    value = (lax.broadcasted_iota(jnp.int32, (256, P_DEV), 0) + 128 * c) % 256
    value = value.astype(jnp.float32)
    slot = col.astype(jnp.float32)
    counts = jnp.zeros((P_DEV, 256), jnp.float32)
    for chunk in range(6):
        ids = here[chunk : chunk + 1, :] if chunk < 4 else beyond[chunk - 4 : chunk - 3, :]
        at = slot + 128.0 * chunk
        member = ((at >= start) & (at < end)).astype(jnp.bfloat16)
        onehot = (value == ids).astype(jnp.bfloat16)
        counts = counts + nt_dot(member, onehot)
    return counts, lens


def two_heads(counts, lens, table):
    times = counts.astype(jnp.bfloat16)
    share = 1.0 / lens
    hide = jnp.where(counts > 0.0, 0.0, NEG)
    pooled = jnp.dot(times, table[:, :256], preferred_element_type=jnp.float32)
    query = (pooled * share).astype(jnp.bfloat16)
    outs = []
    for a in range(2):
        keys, values = (table[:, (i + a) * HD : (i + a + 1) * HD] for i in (2, 4))
        scores = nt_dot(query[:, a * HD : (a + 1) * HD], keys) * SCALE + hide
        expo = jnp.exp(scores - jnp.max(scores, axis=-1, keepdims=True))
        norm = jnp.sum(expo * counts, axis=-1, keepdims=True)
        weights = (expo * (1.0 / norm)).astype(jnp.bfloat16).astype(jnp.float32) * counts
        out = jnp.dot(weights.astype(jnp.bfloat16), values, preferred_element_type=jnp.float32)
        outs.append(out.astype(jnp.bfloat16))
    return jnp.concatenate(outs, axis=1)


def coordinates():
    z, yl, c = (lax.axis_index(name) for name in CTX)
    return z, yl, c, 2 * lax.axis_index("x") + lax.axis_index("yh")


def table_of(tt, own_ref, other_ref):
    return jnp.concatenate([own_ref[tt], other_ref[tt]], axis=0)


def start_kernel(
    ids_ref, lens_ref, table_ref, wq, wk, wv, lq, lk, lv, tables_ref, same_ref, other_ref
):
    z, _, c, _ = coordinates()
    rows = table_ref[pl.ds(pl.multiple_of(VALUES * c, VALUES), VALUES), :]
    for i, ref in enumerate((wq, wk, wv)):
        part = jnp.dot(rows, ref[...], preferred_element_type=jnp.float32).astype(jnp.bfloat16)
        for tt in range(N_TP):
            tables_ref[tt, :, 2 * i * HD : 2 * (i + 1) * HD] = part
    ints = jnp.concatenate(
        [ids_ref[...], lens_ref[...], jnp.zeros((11, HD), jnp.int32)], axis=0
    ).astype(jnp.float32)
    far = z // 8
    for out, a in ((same_ref, far), (other_ref, 1 - far)):
        for i, ref in enumerate((lq, lk, lv)):
            out[i * W_ROWS : (i + 1) * W_ROWS, :] = ref[:, pl.ds(pl.multiple_of(a * HD, HD), HD)]
        out[3 * W_ROWS :, :] = ints.astype(jnp.bfloat16)


def encode_kernel(
    tab_own, tab_other, own_ref, other_ref, gain_ref, q_ref, kv_ref, latent, weight
):
    _, yl, c, t = coordinates()
    parts = [
        byte_counts(4 * z + 2 * yl + c, c, own_ref, other_ref) for z in (t, 2 * N_TP - 1 - t)
    ]
    counts = jnp.concatenate([part[0] for part in parts], axis=0)
    lens = jnp.concatenate([part[1] for part in parts], axis=0)

    def heads(tt, squares):
        out = two_heads(counts, lens, table_of(tt, tab_own, tab_other))
        latent[tt] = out
        wide = out.astype(jnp.float32)
        for ref, core in ((own_ref, c), (other_ref, 1 - c)):
            for b in range(2):
                z = tt if b == 0 else 15 - tt
                for side in range(2):
                    first = pl.multiple_of(W_ROWS * (4 * (z % 2) + 2 * side + core), W_ROWS)
                    for n in range(3):
                        start = (3 * b + n) * W_ROWS
                        weight[z // 2, pl.ds(first, W_ROWS), n * HD : (n + 1) * HD] = ref[
                            2 * tt + side, start : start + W_ROWS, :
                        ]
        return squares + jnp.sum(wide * wide, axis=-1, keepdims=True)

    squares = lax.fori_loop(0, N_TP, heads, jnp.zeros((2 * P_DEV, 1), jnp.float32), unroll=4)
    inverse = lax.rsqrt(squares / 2048.0 + 1e-05)
    total = jnp.zeros((2 * P_DEV, 3 * HD), jnp.float32)
    for tt in range(N_TP):
        gain = gain_ref[:, tt * 256 : (tt + 1) * 256]
        normed = latent[tt].astype(jnp.float32) * inverse * gain
        total = total + jnp.dot(
            normed.astype(jnp.bfloat16), weight[tt], preferred_element_type=jnp.float32
        )
    total = total.astype(jnp.bfloat16)
    q_ref[...] = total[:, :HD]
    for tt in range(N_TP):
        kv_ref[tt] = total[:, HD:]


def latent_kernel(tab_own, tab_other, own_ref, other_ref, out_ref):
    z, yl, c, t = coordinates()
    counts, lens = byte_counts(4 * z + 2 * yl + c, c, own_ref, other_ref)
    out_ref[...] = two_heads(counts, lens, table_of(t, tab_own, tab_other))


def diagonal():
    shape = (P_DEV, P_DEV)
    return lax.broadcasted_iota(jnp.int32, shape, 0) == lax.broadcasted_iota(jnp.int32, shape, 1)


def as_row(column):
    return jnp.sum(jnp.where(diagonal(), column, 0.0), axis=0, keepdims=True)


def as_column(row):
    return jnp.sum(jnp.where(diagonal(), row, 0.0), axis=1, keepdims=True)


def attend_kernel(
    q_own, q_other, kv_own, kv_other, keep_ref, send_ref, scores, query, tops, norms, accs
):
    _, yl, c, t = coordinates()
    size = 2 * P_DEV
    for b in range(2):
        rows = slice(b * P_DEV, (b + 1) * P_DEV)
        query[b, :P_DEV] = q_own[rows]
        query[b, P_DEV:] = q_other[rows]
    tops[...] = jnp.full(tops.shape, NEG, jnp.float32)
    norms[...] = jnp.zeros(norms.shape, jnp.float32)
    accs[...] = jnp.zeros(accs.shape, jnp.float32)
    row = lax.broadcasted_iota(jnp.int32, (size, size), 0)
    col = lax.broadcasted_iota(jnp.int32, (size, size), 1)
    row_at = 256 * jnp.where(row < P_DEV, yl, 1 - yl) + P_DEV * c + row % P_DEV
    col_at = 256 * yl + P_DEV * jnp.where(col < P_DEV, c, 1 - c) + col % P_DEV
    hide = jnp.where(col_at <= row_at, 0.0, NEG)

    def unit(u):
        v = u - N_TP
        near = v <= t
        if u < N_TP:
            return 1, 0, u, False
        tt = jnp.where(near, v, v - 1)
        return jnp.where(near, 0, 1), jnp.where(near, 0, 1), tt, tt == t

    def part(ref, k_block, tt, lanes):
        if isinstance(k_block, int):
            return ref[tt, k_block * P_DEV : (k_block + 1) * P_DEV, lanes]
        return ref[tt, pl.ds(pl.multiple_of(k_block * P_DEV, P_DEV), P_DEV), lanes]

    def first(u):
        q_block, k_block, tt, crossed = unit(u)
        keys = jnp.concatenate(
            [part(ref, k_block, tt, slice(0, HD)) for ref in (kv_own, kv_other)], axis=0
        )
        s = nt_dot(query[q_block], keys) * SCALE
        if u >= N_TP:
            s = s + hide * jnp.where(crossed, 1.0, 0.0)
        scores[u] = s
        tops[q_block] = jnp.maximum(tops[q_block], jnp.maximum(s[:, :HD], s[:, HD:]))

    units = 2 * N_TP + 1
    for u in range(units):
        first(u)
    for b in range(2):
        tops[b] = jnp.broadcast_to(jnp.max(tops[b], axis=-1, keepdims=True), (size, HD))

    def second(u):
        q_block, k_block, tt, _ = unit(u)
        values = jnp.concatenate(
            [part(ref, k_block, tt, slice(HD, 2 * HD)) for ref in (kv_own, kv_other)], axis=0
        )
        top = tops[q_block]
        e = jnp.exp(scores[u] - jnp.concatenate([top, top], axis=1))
        norms[q_block] = norms[q_block] + (e[:, :HD] + e[:, HD:])
        accs[q_block] = accs[q_block] + jnp.dot(
            e.astype(jnp.bfloat16), values, preferred_element_type=jnp.float32
        )

    for u in range(units):
        second(u)
    for half, out in ((0, keep_ref), (1, send_ref)):
        rows = slice(half * P_DEV, (half + 1) * P_DEV)
        stats = [as_row(tops[b, rows, :1]) for b in range(2)]
        stats += [as_row(jnp.sum(norms[b, rows], axis=-1, keepdims=True)) for b in range(2)]
        for b in range(2):
            out[b * P_DEV : (b + 1) * P_DEV, :] = accs[b, rows]
        out[2 * P_DEV :, :] = jnp.concatenate(stats + [jnp.zeros((4, HD), jnp.float32)], axis=0)


def join_kernel(kept_ref, got_ref, same_ref, other_ref):
    z, _, _, _ = coordinates()
    odd = z % 2
    for b in range(2):
        rows = slice(b * P_DEV, (b + 1) * P_DEV)
        at = 2 * P_DEV + b
        top_a, top_b = (as_column(ref[at : at + 1, :]) for ref in (kept_ref, got_ref))
        sum_a, sum_b = (as_column(ref[at + 2 : at + 3, :]) for ref in (kept_ref, got_ref))
        top = jnp.maximum(top_a, top_b)
        a, g = jnp.exp(top_a - top), jnp.exp(top_b - top)
        mixed = (kept_ref[rows] * a + got_ref[rows] * g) / (sum_a * a + sum_b * g)
        mixed = mixed.astype(jnp.bfloat16)

        @pl.when(odd == b)
        def _():
            same_ref[...] = mixed

        @pl.when(odd != b)
        def _():
            other_ref[...] = mixed


def call(body, outs, scratch, flops, *args):
    vmem = pl.BlockSpec(memory_space=pltpu.VMEM)
    return pl.pallas_call(
        body,
        out_shape=[jax.ShapeDtypeStruct(shape, dtype) for shape, dtype in outs],
        in_specs=[vmem] * len(args),
        out_specs=[vmem] * len(outs),
        scratch_shapes=[pltpu.VMEM(shape, dtype) for shape, dtype in scratch],
        compiler_params=pltpu.CompilerParams(vmem_limit_bytes=VMEM),
        cost_estimate=pl.CostEstimate(flops=flops, bytes_accessed=4 << 20, transcendentals=1 << 20),
    )(*args)


BF, F32 = jnp.bfloat16, jnp.float32


def run_start(*args):
    outs = [((N_TP, VALUES, 6 * HD), BF)] + [((3 * W_ROWS + 16, HD), BF)] * 2
    return call(start_kernel, outs, [], 1 << 28, *args)


def run_encode(*args):
    outs = [((2 * P_DEV, HD), BF), ((N_TP, 2 * P_DEV, 2 * HD), BF)]
    scratch = [((N_TP, 256, 256), BF), ((N_TP, 256, 3 * HD), BF)]
    return call(encode_kernel, outs, scratch, 1 << 30, *args)


def run_latent(*args):
    return call(latent_kernel, [((P_DEV, 256), BF)], [], 1 << 26, *args)[0]


def run_attend(*args):
    block = (2, 2 * P_DEV, HD)
    scratch = [((2 * N_TP + 1, 2 * P_DEV, 2 * P_DEV), F32), (block, BF)] + [(block, F32)] * 3
    return call(attend_kernel, [((PART, HD), F32)] * 2, scratch, 1 << 30, *args)


def run_join(*args):
    return call(join_kernel, [((P_DEV, HD), BF)] * 2, [], 1 << 20, *args)


def on_device(
    byte_ids,
    patch_lens,
    byte_table,
    wq_cross,
    wk_cross,
    wv_cross,
    norm_gain,
    wq_latent,
    wk_latent,
    wv_latent,
):
    z = lax.axis_index("z")
    far, odd = z >= 8, z % 2 == 1
    swap = [(0, 1), (1, 0)]
    same, other = turns()

    tables, to_same, to_other = run_start(
        byte_ids.reshape(4, HD),
        patch_lens.reshape(1, HD),
        byte_table,
        wq_cross,
        wk_cross,
        wv_cross,
        wq_latent,
        wk_latent,
        wv_latent,
    )
    got_same = lax.ppermute(to_same, TURN, same)
    got_other = lax.ppermute(to_other, TURN, other)
    tab_own = lax.all_to_all(tables, TP, 0, 0)
    tab_other = lax.ppermute(tab_own, "c", swap)
    near = jnp.where(odd, got_other, got_same)
    away = jnp.where(odd, got_same, got_other)
    cut = 3 * W_ROWS
    message = jnp.concatenate([near[:cut], away[:cut], near[cut:], away[cut:]], axis=0)
    msg_own = to_all(message, PLANE, 16)
    msg_other = lax.ppermute(msg_own, "c", swap)

    q, kv = run_encode(tab_own, tab_other, msg_own, msg_other, norm_gain.reshape(1, 2048))
    q_other = lax.ppermute(q, "yl", swap)
    kv_own = lax.all_to_all(kv, TP, 0, 0)
    kv_other = lax.ppermute(kv_own, "c", swap)
    kept, sent = run_attend(q, q_other, kv_own, kv_other)
    head_same, head_other = run_join(kept, lax.ppermute(sent, "yl", swap))
    head_same = lax.ppermute(head_same, TURN, back(same))
    head_other = lax.ppermute(head_other, TURN, back(other))
    patch_latent = run_latent(tab_own, tab_other, msg_own, msg_other)
    latent_mixed = jnp.concatenate(
        [jnp.where(far, head_other, head_same), jnp.where(far, head_same, head_other)], axis=1
    )
    return (patch_latent, latent_mixed)


def solution(mesh):
    fine = Mesh(mesh.devices.reshape(16, 2, 2, 4, 2), ("z", "yl", "c", "x", "yh"))
    return jax.shard_map(
        on_device,
        mesh=fine,
        in_specs=(
            P(CTX),
            P(CTX),
            P(),
            P(None, TP),
            P(None, TP),
            P(None, TP),
            P(),
            P(CTX, TP),
            P(CTX, TP),
            P(CTX, TP),
        ),
        out_specs=(P(CTX, TP), P(CTX, TP)),
        check_vma=False,
    )
```

```python
import math

import jax
import jax.numpy as jnp
from jax import lax
from jax.experimental import pallas as pl
from jax.experimental.pallas import tpu as pltpu
from jax.sharding import Mesh
from jax.sharding import PartitionSpec as P

HD = 128
SCALE = 1.0 / math.sqrt(HD)
NEG = -1e30
N_CTX = 64
N_TP = 8
BYTES_DEV = 512
P_DEV = 128
W_ROWS = 32
VALUES = 128
ROWS = 2 * 3 * W_ROWS
MSG = ROWS + 2 * 16
PART = P_DEV + 8
VMEM = 20 * 1024 * 1024

CTX = ("z", "yl", "c")
TP = ("x", "yh")
PLANE = ("x", "yh", "yl")
TURN = ("z", "yl", "x", "yh")


def turned(index, yl):
    return index + yl * (N_TP - 1 - 2 * index)


def flat(z, yl, t):
    return (z * 2 + yl) * N_TP + t


def turns():
    same, other = [], []
    for z in range(16):
        for yl in range(2):
            for t in range(N_TP):
                tt = turned(z // 2, yl)
                same.append((flat(z, yl, t), flat(2 * t + z % 2, yl, tt)))
                other.append((flat(z, yl, t), flat(2 * t + 1 - z % 2, yl, tt)))
    return same, other


def back(pairs):
    return [(target, source) for source, target in pairs]


def to_all(value, axes, count):
    return lax.all_to_all(jnp.broadcast_to(value[None], (count, *value.shape)), axes, 0, 0)


def nt_dot(a, b):
    return lax.dot_general(a, b, (((1,), (1,)), ((), ())), preferred_element_type=jnp.float32)


def lens_before(d, c, own_ref, other_ref):
    total = jnp.zeros((), jnp.float32)
    for ref, core in ((own_ref, c), (other_ref, 1 - c)):
        for b in range(2):
            tiles = ref[:, ROWS + 16 * b : ROWS + 16 * (b + 1), :].astype(jnp.float32)
            unit, row = (lax.broadcasted_iota(jnp.int32, tiles.shape, i) for i in range(2))
            z = 2 * turned(unit // 2, unit % 2) + b
            place = 4 * z + 2 * (unit % 2) + core
            total = total + jnp.sum(jnp.where((row == 4) & (place < d), tiles, 0.0))
    return total


def byte_counts(d, c, own_ref, other_ref):
    follow = jnp.where(d < N_CTX - 1, d + 1, d - 1)

    def tile(ref, place):
        z, yl = place // 4, (place // 2) % 2
        unit = 2 * turned(z // 2, yl) + yl
        first = pl.multiple_of(ROWS + 16 * (z % 2), 16)
        return ref[unit, pl.ds(first, 16), :].astype(jnp.float32)

    here, beyond = tile(own_ref, d), tile(other_ref, follow)
    begin = lens_before(d, c, own_ref, other_ref) - (d * BYTES_DEV).astype(jnp.float32)
    lens_row = here[4:5, :]
    row = lax.broadcasted_iota(jnp.int32, (P_DEV, P_DEV), 0)
    col = lax.broadcasted_iota(jnp.int32, (P_DEV, P_DEV), 1)
    lens = jnp.sum(jnp.where(col == row, lens_row, 0.0), axis=1, keepdims=True)
    start = begin + jnp.sum(jnp.where(col < row, lens_row, 0.0), axis=1, keepdims=True)
    end = start + lens
    value = (lax.broadcasted_iota(jnp.int32, (256, P_DEV), 0) + 128 * c) % 256
    value = value.astype(jnp.float32)
    slot = col.astype(jnp.float32)
    counts = jnp.zeros((P_DEV, 256), jnp.float32)
    for chunk in range(6):
        ids = here[chunk : chunk + 1, :] if chunk < 4 else beyond[chunk - 4 : chunk - 3, :]
        at = slot + 128.0 * chunk
        member = ((at >= start) & (at < end)).astype(jnp.bfloat16)
        onehot = (value == ids).astype(jnp.bfloat16)
        counts = counts + nt_dot(member, onehot)
    return counts, lens


def two_heads(counts, lens, table):
    times = counts.astype(jnp.bfloat16)
    share = 1.0 / lens
    hide = jnp.where(counts > 0.0, 0.0, NEG)
    pooled = jnp.dot(times, table[:, :256], preferred_element_type=jnp.float32)
    query = (pooled * share).astype(jnp.bfloat16)
    outs = []
    for a in range(2):
        keys, values = (table[:, (i + a) * HD : (i + a + 1) * HD] for i in (2, 4))
        scores = nt_dot(query[:, a * HD : (a + 1) * HD], keys) * SCALE + hide
        expo = jnp.exp(scores - jnp.max(scores, axis=-1, keepdims=True))
        norm = jnp.sum(expo * counts, axis=-1, keepdims=True)
        weights = (expo * (1.0 / norm)).astype(jnp.bfloat16).astype(jnp.float32) * counts
        out = jnp.dot(weights.astype(jnp.bfloat16), values, preferred_element_type=jnp.float32)
        outs.append(out.astype(jnp.bfloat16))
    return jnp.concatenate(outs, axis=1)


def coordinates():
    z, yl, c = (lax.axis_index(name) for name in CTX)
    return z, yl, c, 2 * lax.axis_index("x") + lax.axis_index("yh")


def table_of(tt, own_ref, other_ref):
    return jnp.concatenate([own_ref[tt], other_ref[tt]], axis=0)


def start_kernel(
    ids_ref, lens_ref, table_ref, wq, wk, wv, lq, lk, lv, tables_ref, same_ref, other_ref
):
    z, _, c, _ = coordinates()
    rows = table_ref[pl.ds(pl.multiple_of(VALUES * c, VALUES), VALUES), :]
    for i, ref in enumerate((wq, wk, wv)):
        part = jnp.dot(rows, ref[...], preferred_element_type=jnp.float32).astype(jnp.bfloat16)
        for tt in range(N_TP):
            tables_ref[tt, :, 2 * i * HD : 2 * (i + 1) * HD] = part
    ints = jnp.concatenate(
        [ids_ref[...], lens_ref[...], jnp.zeros((11, HD), jnp.int32)], axis=0
    ).astype(jnp.float32)
    odd = z % 2
    for out, a in ((same_ref, odd), (other_ref, 1 - odd)):
        for i, ref in enumerate((lq, lk, lv)):
            out[i * W_ROWS : (i + 1) * W_ROWS, :] = ref[:, pl.ds(pl.multiple_of(a * HD, HD), HD)]
        out[3 * W_ROWS :, :] = ints.astype(jnp.bfloat16)


def encode_kernel(
    tab_own, tab_other, own_ref, other_ref, gain_ref, q_ref, kv_ref, latent, weight
):
    _, yl, c, t = coordinates()
    first_z = 2 * turned(t, yl)
    parts = [
        byte_counts(4 * z + 2 * yl + c, c, own_ref, other_ref) for z in (first_z, first_z + 1)
    ]
    counts = jnp.concatenate([part[0] for part in parts], axis=0)
    lens = jnp.concatenate([part[1] for part in parts], axis=0)

    def heads(tt, squares):
        out = two_heads(counts, lens, table_of(tt, tab_own, tab_other))
        latent[tt] = out
        wide = out.astype(jnp.float32)
        for ref, core in ((own_ref, c), (other_ref, 1 - c)):
            for b in range(2):
                for side in range(2):
                    first = pl.multiple_of(W_ROWS * (4 * b + 2 * side + core), W_ROWS)
                    for n in range(3):
                        start = (3 * b + n) * W_ROWS
                        weight[turned(tt, side), pl.ds(first, W_ROWS), n * HD : (n + 1) * HD] = ref[
                            2 * tt + side, start : start + W_ROWS, :
                        ]
        return squares + jnp.sum(wide * wide, axis=-1, keepdims=True)

    squares = lax.fori_loop(0, N_TP, heads, jnp.zeros((2 * P_DEV, 1), jnp.float32), unroll=4)
    inverse = lax.rsqrt(squares / 2048.0 + 1e-05)
    total = jnp.zeros((2 * P_DEV, 3 * HD), jnp.float32)
    for tt in range(N_TP):
        gain = gain_ref[:, tt * 256 : (tt + 1) * 256]
        normed = latent[tt].astype(jnp.float32) * inverse * gain
        total = total + jnp.dot(
            normed.astype(jnp.bfloat16), weight[tt], preferred_element_type=jnp.float32
        )
    total = total.astype(jnp.bfloat16)
    q_ref[...] = total[:, :HD]
    for tt in range(N_TP):
        kv_ref[tt] = total[:, HD:]


def latent_kernel(tab_own, tab_other, own_ref, other_ref, out_ref):
    z, yl, c, t = coordinates()
    counts, lens = byte_counts(4 * z + 2 * yl + c, c, own_ref, other_ref)
    out_ref[...] = two_heads(counts, lens, table_of(t, tab_own, tab_other))


def diagonal():
    shape = (P_DEV, P_DEV)
    return lax.broadcasted_iota(jnp.int32, shape, 0) == lax.broadcasted_iota(jnp.int32, shape, 1)


def as_row(column):
    return jnp.sum(jnp.where(diagonal(), column, 0.0), axis=0, keepdims=True)


def as_column(row):
    return jnp.sum(jnp.where(diagonal(), row, 0.0), axis=1, keepdims=True)


def attend_kernel(
    q_own,
    q_other,
    kv_own,
    kv_other,
    keep_ref,
    to_yl_ref,
    to_z_ref,
    to_both_ref,
    scores,
    query,
    tops,
    norms,
    accs,
):
    z, yl, c, t = coordinates()
    size = 2 * P_DEV
    query[yl] = q_own[...]
    query[1 - yl] = q_other[...]
    tops[...] = jnp.full(tops.shape, NEG, jnp.float32)
    norms[...] = jnp.zeros(norms.shape, jnp.float32)
    accs[...] = jnp.zeros(accs.shape, jnp.float32)
    row = lax.broadcasted_iota(jnp.int32, (size, size), 0)
    col = lax.broadcasted_iota(jnp.int32, (size, size), 1)
    behind = 512 * (row // P_DEV - col // P_DEV) + row % P_DEV - col % P_DEV

    def hide(q_yl, core):
        return jnp.where(behind + 256 * (q_yl - yl) + P_DEV * (c - core) >= 0, 0.0, NEG)

    units = N_TP + 1

    def unit(u):
        if u == N_TP:
            return 1, turned(N_TP - 1 - t, yl)
        first = u <= t
        return jnp.where(first, 0, 1), turned(jnp.where(first, u, u - t - 1), yl)

    sides = ((kv_own, c), (kv_other, 1 - c))
    for u in range(units):
        q_yl, tt = unit(u)
        best = tops[q_yl]
        for i, (ref, core) in enumerate(sides):
            s = nt_dot(query[q_yl], ref[tt, :, :HD]) * SCALE
            if u == N_TP:
                s = s + hide(1, core)
            else:
                s = s + hide(0, core) * jnp.where(u == t, 1.0, 0.0)
            scores[u, i] = s
            best = jnp.maximum(best, jnp.maximum(s[:, :HD], s[:, HD:]))
        tops[q_yl] = best
    for b in range(2):
        tops[b] = jnp.broadcast_to(jnp.max(tops[b], axis=-1, keepdims=True), (size, HD))
    for u in range(units):
        q_yl, tt = unit(u)
        top = tops[q_yl]
        top = jnp.concatenate([top, top], axis=1)
        norm, acc = norms[q_yl], accs[q_yl]
        for i, (ref, _) in enumerate(sides):
            e = jnp.exp(scores[u, i] - top)
            norm = norm + (e[:, :HD] + e[:, HD:])
            acc = acc + jnp.dot(
                e.astype(jnp.bfloat16), ref[tt, :, HD:], preferred_element_type=jnp.float32
            )
        norms[q_yl] = norm
        accs[q_yl] = acc
    odd = z % 2
    for out, q_yl, b in (
        (keep_ref, yl, odd),
        (to_yl_ref, 1 - yl, odd),
        (to_z_ref, yl, 1 - odd),
        (to_both_ref, 1 - yl, 1 - odd),
    ):
        rows = pl.ds(pl.multiple_of(b * P_DEV, P_DEV), P_DEV)
        out[:P_DEV, :] = accs[q_yl, rows, :]
        total = jnp.sum(norms[q_yl, rows, :], axis=-1, keepdims=True)
        stats = [as_row(tops[q_yl, rows, :][:, :1]), as_row(total), jnp.zeros((6, HD), jnp.float32)]
        out[P_DEV:, :] = jnp.concatenate(stats, axis=0)


def join_kernel(kept, got_yl, got_z, got_both, out_ref):
    z, _, _, _ = coordinates()
    odd = z % 2
    for a, pair in ((odd, (kept, got_yl)), (1 - odd, (got_z, got_both))):
        tops = [as_column(ref[P_DEV : P_DEV + 1, :]) for ref in pair]
        sums = [as_column(ref[P_DEV + 1 : P_DEV + 2, :]) for ref in pair]
        top = jnp.maximum(*tops)
        scale = [jnp.exp(part - top) for part in tops]
        mixed = pair[0][:P_DEV, :] * scale[0] + pair[1][:P_DEV, :] * scale[1]
        mixed = mixed / (sums[0] * scale[0] + sums[1] * scale[1])
        out_ref[:, pl.ds(pl.multiple_of(a * HD, HD), HD)] = mixed.astype(jnp.bfloat16)


def call(body, outs, scratch, flops, *args, limit=VMEM):
    vmem = pl.BlockSpec(memory_space=pltpu.VMEM)
    return pl.pallas_call(
        body,
        out_shape=[jax.ShapeDtypeStruct(shape, dtype) for shape, dtype in outs],
        in_specs=[vmem] * len(args),
        out_specs=[vmem] * len(outs),
        scratch_shapes=[pltpu.VMEM(shape, dtype) for shape, dtype in scratch],
        compiler_params=pltpu.CompilerParams(vmem_limit_bytes=limit),
        cost_estimate=pl.CostEstimate(flops=flops, bytes_accessed=4 << 20, transcendentals=1 << 20),
    )(*args)


BF, F32 = jnp.bfloat16, jnp.float32


def run_start(*args):
    outs = [((N_TP, VALUES, 6 * HD), BF)] + [((3 * W_ROWS + 16, HD), BF)] * 2
    return call(start_kernel, outs, [], 1 << 28, *args, limit=56 << 20)


def run_encode(*args):
    outs = [((2 * P_DEV, HD), BF), ((N_TP, 2 * P_DEV, 2 * HD), BF)]
    scratch = [((N_TP, 256, 256), BF), ((N_TP, 256, 3 * HD), BF)]
    return call(encode_kernel, outs, scratch, 1 << 30, *args)


def run_latent(*args):
    return call(latent_kernel, [((P_DEV, 256), BF)], [], 1 << 26, *args)[0]


def run_attend(*args):
    size = 2 * P_DEV
    block = (2, size, HD)
    scratch = [((N_TP + 1, 2, size, size), F32), (block, BF)] + [(block, F32)] * 3
    return call(attend_kernel, [((PART, HD), F32)] * 4, scratch, 1 << 30, *args)


def run_join(*args):
    return call(join_kernel, [((P_DEV, 2 * HD), BF)], [], 1 << 20, *args)[0]


def on_device(
    byte_ids,
    patch_lens,
    byte_table,
    wq_cross,
    wk_cross,
    wv_cross,
    norm_gain,
    wq_latent,
    wk_latent,
    wv_latent,
):
    z = lax.axis_index("z")
    odd = z % 2 == 1
    swap = [(0, 1), (1, 0)]
    same, other = turns()

    tables, to_same, to_other = run_start(
        byte_ids.reshape(4, HD),
        patch_lens.reshape(1, HD),
        byte_table,
        wq_cross,
        wk_cross,
        wv_cross,
        wq_latent,
        wk_latent,
        wv_latent,
    )
    got_same = lax.ppermute(to_same, TURN, same)
    got_other = lax.ppermute(to_other, TURN, other)
    tab_own = lax.all_to_all(tables, TP, 0, 0)
    tab_other = lax.ppermute(tab_own, "c", swap)
    near = jnp.where(odd, got_other, got_same)
    away = jnp.where(odd, got_same, got_other)
    cut = 3 * W_ROWS
    message = jnp.concatenate([near[:cut], away[:cut], near[cut:], away[cut:]], axis=0)
    msg_own = to_all(message, PLANE, 16)
    msg_other = lax.ppermute(msg_own, "c", swap)

    q, kv = run_encode(tab_own, tab_other, msg_own, msg_other, norm_gain.reshape(1, 2048))
    q_other = lax.ppermute(q, "yl", swap)
    kv_own = lax.all_to_all(kv, TP, 0, 0)
    kv_own, q_other = lax.optimization_barrier((kv_own, q_other))
    kv_other = lax.ppermute(kv_own, "c", swap)
    kept, to_yl, to_z, to_both = run_attend(q, q_other, kv_own, kv_other)
    got_both = lax.ppermute(to_both, ("z", "yl"), [(i, i ^ 3) for i in range(32)])
    got_z = lax.ppermute(to_z, "z", [(i, i ^ 1) for i in range(16)])
    got_yl = lax.ppermute(to_yl, "yl", swap)
    mixed = run_join(kept, got_yl, got_z, got_both)
    latent_mixed = lax.ppermute(mixed, TURN, back(same))
    patch_latent = run_latent(tab_own, tab_other, msg_own, msg_other)
    return (patch_latent, latent_mixed)


def solution(mesh):
    fine = Mesh(mesh.devices.reshape(16, 2, 2, 4, 2), ("z", "yl", "c", "x", "yh"))
    return jax.shard_map(
        on_device,
        mesh=fine,
        in_specs=(
            P(CTX),
            P(CTX),
            P(),
            P(None, TP),
            P(None, TP),
            P(None, TP),
            P(),
            P(CTX, TP),
            P(CTX, TP),
            P(CTX, TP),
        ),
        out_specs=(P(CTX, TP), P(CTX, TP)),
        check_vma=False,
    )
```

```python
import math

import jax
import jax.numpy as jnp
from jax import lax
from jax.experimental import pallas as pl
from jax.experimental.pallas import tpu as pltpu
from jax.sharding import Mesh
from jax.sharding import PartitionSpec as P

HD = 128
SCALE = 1.0 / math.sqrt(HD)
NEG = -1e30
N_CTX = 64
N_TP = 8
BYTES_DEV = 512
P_DEV = 128
W_ROWS = 32
VALUES = 128
ROWS = 3 * W_ROWS
MSG = ROWS + 16
PART = P_DEV + 8
VMEM = 20 * 1024 * 1024

Z = ("zh", "zl")
CTX = (*Z, "yl", "c")
PAIR = ("zl", "yl")
TP = ("x", "yh")
PLANES = ("zl", "x", "yh", "yl")
TURN = (*Z, "yl", "x", "yh")


def turned(index, yl):
    return index + yl * (N_TP - 1 - 2 * index)


def flat(z, yl, t):
    return (z * 2 + yl) * N_TP + t


def turns():
    return [
        (flat(z, yl, t), flat(2 * t + z % 2, yl, turned(z // 2, yl)))
        for z in range(16)
        for yl in range(2)
        for t in range(N_TP)
    ]


def nt_dot(a, b):
    return lax.dot_general(a, b, (((1,), (1,)), ((), ())), preferred_element_type=jnp.float32)


def lens_before(d, c, own_ref, other_ref):
    total = jnp.zeros((), jnp.float32)
    for ref, core in ((own_ref, c), (other_ref, 1 - c)):
        tiles = ref[:, ROWS:, :].astype(jnp.float32)
        slot, row = (lax.broadcasted_iota(jnp.int32, tiles.shape, i) for i in range(2))
        unit, b = slot % 16, slot // 16
        place = 8 * turned(unit // 2, unit % 2) + 4 * b + 2 * (unit % 2) + core
        total = total + jnp.sum(jnp.where((row == 4) & (place < d), tiles, 0.0))
    return total


def byte_counts(d, c, own_ref, other_ref):
    follow = jnp.where(d < N_CTX - 1, d + 1, d - 1)

    def tile(ref, place):
        z, yl = place // 4, (place // 2) % 2
        unit = 2 * turned(z // 2, yl) + yl
        return ref[16 * (z % 2) + unit, ROWS:, :].astype(jnp.float32)

    here, beyond = tile(own_ref, d), tile(other_ref, follow)
    begin = lens_before(d, c, own_ref, other_ref) - (d * BYTES_DEV).astype(jnp.float32)
    lens_row = here[4:5, :]
    row = lax.broadcasted_iota(jnp.int32, (P_DEV, P_DEV), 0)
    col = lax.broadcasted_iota(jnp.int32, (P_DEV, P_DEV), 1)
    lens = jnp.sum(jnp.where(col == row, lens_row, 0.0), axis=1, keepdims=True)
    start = begin + jnp.sum(jnp.where(col < row, lens_row, 0.0), axis=1, keepdims=True)
    end = start + lens
    value = lax.broadcasted_iota(jnp.int32, (256, P_DEV), 0) ^ (VALUES * c)
    value = value.astype(jnp.float32)
    slot = col.astype(jnp.float32)
    counts = jnp.zeros((P_DEV, 256), jnp.float32)
    for chunk in range(6):
        ids = here[chunk : chunk + 1, :] if chunk < 4 else beyond[chunk - 4 : chunk - 3, :]
        at = slot + 128.0 * chunk
        member = ((at >= start) & (at < end)).astype(jnp.bfloat16)
        onehot = (value == ids).astype(jnp.bfloat16)
        counts = counts + nt_dot(member, onehot)
    return counts, lens


def two_heads(counts, lens, table):
    times = counts.astype(jnp.bfloat16)
    share = 1.0 / lens
    hide = jnp.where(counts > 0.0, 0.0, NEG)
    pooled = jnp.dot(times, table[:, :256], preferred_element_type=jnp.float32)
    query = (pooled * share).astype(jnp.bfloat16)
    outs = []
    for a in range(2):
        keys, values = (table[:, (i + a) * HD : (i + a + 1) * HD] for i in (2, 4))
        scores = nt_dot(query[:, a * HD : (a + 1) * HD], keys) * SCALE + hide
        expo = jnp.exp(scores - jnp.max(scores, axis=-1, keepdims=True))
        norm = jnp.sum(expo * counts, axis=-1, keepdims=True)
        weights = (expo * (1.0 / norm)).astype(jnp.bfloat16).astype(jnp.float32) * counts
        out = jnp.dot(weights.astype(jnp.bfloat16), values, preferred_element_type=jnp.float32)
        outs.append(out.astype(jnp.bfloat16))
    return jnp.concatenate(outs, axis=1)


def coordinates():
    zh, zl, yl, c = (lax.axis_index(name) for name in CTX)
    return 2 * zh + zl, yl, c, 2 * lax.axis_index("x") + lax.axis_index("yh")


def table_of(tt, refs):
    return jnp.concatenate([ref[tt] for ref in refs], axis=0)


def start_kernel(
    ids_ref, lens_ref, table_ref, wq, wk, wv, lq, lk, lv, tables_ref, message_ref
):
    _, _, c, _ = coordinates()
    first = pl.multiple_of(VALUES * c, VALUES)
    rows = table_ref[pl.ds(first, VALUES), :]
    for i, ref in enumerate((wq, wk, wv)):
        part = jnp.dot(rows, ref[...], preferred_element_type=jnp.float32).astype(jnp.bfloat16)
        for tt in range(N_TP):
            tables_ref[tt, :, 2 * i * HD : 2 * (i + 1) * HD] = part
    ints = jnp.concatenate(
        [ids_ref[...], lens_ref[...], jnp.zeros((11, HD), jnp.int32)], axis=0
    ).astype(jnp.float32)
    for a in range(2):
        for i, ref in enumerate((lq, lk, lv)):
            message_ref[a, i * W_ROWS : (i + 1) * W_ROWS, :] = ref[:, a * HD : (a + 1) * HD]
        message_ref[a, ROWS:, :] = ints.astype(jnp.bfloat16)


def encode_kernel(*refs):
    tables = refs[:2]
    own_ref, other_ref, gain_ref, q_ref, kv_ref, latent, weight = refs[2:]
    _, yl, c, t = coordinates()
    first_z = 2 * turned(t, yl)
    parts = [
        byte_counts(4 * z + 2 * yl + c, c, own_ref, other_ref)
        for z in (first_z, first_z + 1)
    ]
    counts = jnp.concatenate([part[0] for part in parts], axis=0)
    lens = jnp.concatenate([part[1] for part in parts], axis=0)

    def heads(tt, squares):
        out = two_heads(counts, lens, table_of(tt, tables))
        latent[tt] = out
        wide = out.astype(jnp.float32)
        for ref, core in ((own_ref, c), (other_ref, 1 - c)):
            for b in range(2):
                for side in range(2):
                    first = pl.multiple_of(W_ROWS * (4 * b + 2 * side + core), W_ROWS)
                    for n in range(3):
                        weight[turned(tt, side), pl.ds(first, W_ROWS), n * HD : (n + 1) * HD] = ref[
                            16 * b + 2 * tt + side, n * W_ROWS : (n + 1) * W_ROWS, :
                        ]
        return squares + jnp.sum(wide * wide, axis=-1, keepdims=True)

    squares = lax.fori_loop(0, N_TP, heads, jnp.zeros((2 * P_DEV, 1), jnp.float32), unroll=4)
    inverse = lax.rsqrt(squares / 2048.0 + 1e-05)
    total = jnp.zeros((2 * P_DEV, 3 * HD), jnp.float32)
    for tt in range(N_TP):
        gain = gain_ref[:, tt * 256 : (tt + 1) * 256]
        normed = latent[tt].astype(jnp.float32) * inverse * gain
        total = total + jnp.dot(
            normed.astype(jnp.bfloat16), weight[tt], preferred_element_type=jnp.float32
        )
    total = total.astype(jnp.bfloat16)
    q_ref[...] = total[:, :HD]
    for tt in range(N_TP):
        kv_ref[tt] = total[:, HD:]


def latent_kernel(*refs):
    own_ref, other_ref, out_ref = refs[2:]
    z, yl, c, t = coordinates()
    counts, lens = byte_counts(4 * z + 2 * yl + c, c, own_ref, other_ref)
    out_ref[...] = two_heads(counts, lens, table_of(t, refs[:2]))


def diagonal():
    shape = (P_DEV, P_DEV)
    return lax.broadcasted_iota(jnp.int32, shape, 0) == lax.broadcasted_iota(jnp.int32, shape, 1)


def as_row(column):
    return jnp.sum(jnp.where(diagonal(), column, 0.0), axis=0, keepdims=True)


def as_column(row):
    return jnp.sum(jnp.where(diagonal(), row, 0.0), axis=1, keepdims=True)


def attend_kernel(
    q_own,
    q_other,
    kv_own,
    kv_other,
    out_ref,
    scores,
    query,
    tops,
    norms,
    accs,
):
    _, yl, c, t = coordinates()
    size = 2 * P_DEV
    query[yl] = q_own[...]
    query[1 - yl] = q_other[...]
    tops[...] = jnp.full(tops.shape, NEG, jnp.float32)
    norms[...] = jnp.zeros(norms.shape, jnp.float32)
    accs[...] = jnp.zeros(accs.shape, jnp.float32)
    row = lax.broadcasted_iota(jnp.int32, (size, size), 0)
    col = lax.broadcasted_iota(jnp.int32, (size, size), 1)
    behind = 512 * (row // P_DEV - col // P_DEV) + row % P_DEV - col % P_DEV

    def hide(q_yl, core):
        return jnp.where(behind + 256 * (q_yl - yl) + P_DEV * (c - core) >= 0, 0.0, NEG)

    units = N_TP + 1

    def unit(u):
        if u == N_TP:
            return 1, turned(N_TP - 1 - t, yl)
        first = u <= t
        return jnp.where(first, 0, 1), turned(jnp.where(first, u, u - t - 1), yl)

    sides = ((kv_own, c), (kv_other, 1 - c))
    for u in range(units):
        q_yl, tt = unit(u)
        best = tops[q_yl]
        for i, (ref, core) in enumerate(sides):
            s = nt_dot(query[q_yl], ref[tt, :, :HD]) * SCALE
            if u == N_TP:
                s = s + hide(1, core)
            else:
                s = s + hide(0, core) * jnp.where(u == t, 1.0, 0.0)
            scores[u, i] = s
            best = jnp.maximum(best, jnp.maximum(s[:, :HD], s[:, HD:]))
        tops[q_yl] = best
    for b in range(2):
        tops[b] = jnp.broadcast_to(jnp.max(tops[b], axis=-1, keepdims=True), (size, HD))
    for u in range(units):
        q_yl, tt = unit(u)
        top = tops[q_yl]
        top = jnp.concatenate([top, top], axis=1)
        norm, acc = norms[q_yl], accs[q_yl]
        for i, (ref, _) in enumerate(sides):
            e = jnp.exp(scores[u, i] - top)
            norm = norm + (e[:, :HD] + e[:, HD:])
            acc = acc + jnp.dot(
                e.astype(jnp.bfloat16), ref[tt, :, HD:], preferred_element_type=jnp.float32
            )
        norms[q_yl] = norm
        accs[q_yl] = acc
    for b in range(2):
        rows = slice(b * P_DEV, (b + 1) * P_DEV)
        for q_yl in range(2):
            slot = 2 * b + q_yl
            out_ref[slot, :P_DEV, :] = accs[q_yl, rows, :]
            total = jnp.sum(norms[q_yl, rows, :], axis=-1, keepdims=True)
            stats = [as_row(tops[q_yl, rows, :1]), as_row(total), jnp.zeros((6, HD), jnp.float32)]
            out_ref[slot, P_DEV:, :] = jnp.concatenate(stats, axis=0)


def join_kernel(part_ref, out_ref):
    for a in range(2):
        slots = (2 * a, 2 * a + 1)
        tops = [as_column(part_ref[i, P_DEV : P_DEV + 1, :]) for i in slots]
        sums = [as_column(part_ref[i, P_DEV + 1 : P_DEV + 2, :]) for i in slots]
        top = jnp.maximum(*tops)
        scale = [jnp.exp(part - top) for part in tops]
        mixed = part_ref[slots[0], :P_DEV, :] * scale[0] + part_ref[slots[1], :P_DEV, :] * scale[1]
        mixed = mixed / (sums[0] * scale[0] + sums[1] * scale[1])
        out_ref[:, a * HD : (a + 1) * HD] = mixed.astype(jnp.bfloat16)


def call(body, outs, scratch, flops, *args, limit=VMEM):
    vmem = pl.BlockSpec(memory_space=pltpu.VMEM)
    return pl.pallas_call(
        body,
        out_shape=[jax.ShapeDtypeStruct(shape, dtype) for shape, dtype in outs],
        in_specs=[vmem] * len(args),
        out_specs=[vmem] * len(outs),
        scratch_shapes=[pltpu.VMEM(shape, dtype) for shape, dtype in scratch],
        compiler_params=pltpu.CompilerParams(vmem_limit_bytes=limit),
        cost_estimate=pl.CostEstimate(flops=flops, bytes_accessed=4 << 20, transcendentals=1 << 20),
    )(*args)


BF, F32 = jnp.bfloat16, jnp.float32


def run_start(*args):
    outs = [((N_TP, VALUES, 6 * HD), BF), ((2, MSG, HD), BF)]
    return call(start_kernel, outs, [], 1 << 28, *args, limit=56 << 20)


def run_encode(*args):
    outs = [((2 * P_DEV, HD), BF), ((N_TP, 2 * P_DEV, 2 * HD), BF)]
    scratch = [((N_TP, 256, 256), BF), ((N_TP, 256, 3 * HD), BF)]
    return call(encode_kernel, outs, scratch, 1 << 30, *args)


def run_latent(*args):
    return call(latent_kernel, [((P_DEV, 256), BF)], [], 1 << 26, *args)[0]


def run_attend(*args):
    size = 2 * P_DEV
    block = (2, size, HD)
    scratch = [((N_TP + 1, 2, size, size), F32), (block, BF)] + [(block, F32)] * 3
    return call(attend_kernel, [((4, PART, HD), F32)], scratch, 1 << 30, *args)[0]


def run_join(*args):
    return call(join_kernel, [((P_DEV, 2 * HD), BF)], [], 1 << 20, *args)[0]


def on_device(
    byte_ids,
    patch_lens,
    byte_table,
    wq_cross,
    wk_cross,
    wv_cross,
    norm_gain,
    wq_latent,
    wk_latent,
    wv_latent,
):
    swap = [(0, 1), (1, 0)]
    turn = turns()

    tables, message = run_start(
        byte_ids.reshape(4, HD),
        patch_lens.reshape(1, HD),
        byte_table,
        wq_cross,
        wk_cross,
        wv_cross,
        wq_latent,
        wk_latent,
        wv_latent,
    )
    message = lax.ppermute(message, TURN, turn)
    tab_own = lax.all_to_all(tables, TP, 0, 0)
    byte_tables = (tab_own, lax.ppermute(tab_own, "c", swap))
    message = jnp.broadcast_to(message[:, None], (2, 16, MSG, HD)).reshape(32, MSG, HD)
    msg_own = lax.all_to_all(message, PLANES, 0, 0, tiled=True)
    msg_other = lax.ppermute(msg_own, "c", swap)

    q, kv = run_encode(*byte_tables, msg_own, msg_other, norm_gain.reshape(1, 2048))
    q_other = lax.ppermute(q, "yl", swap)
    kv_own = lax.all_to_all(kv, TP, 0, 0)
    kv_own, q_other = lax.optimization_barrier((kv_own, q_other))
    kv_other = lax.ppermute(kv_own, "c", swap)
    parts = run_attend(q, q_other, kv_own, kv_other)
    mixed = run_join(lax.all_to_all(parts, PAIR, 0, 0))
    latent_mixed = lax.ppermute(mixed, TURN, [(target, source) for source, target in turn])
    patch_latent = run_latent(*byte_tables, msg_own, msg_other)
    return (patch_latent, latent_mixed)


def solution(mesh):
    fine = Mesh(mesh.devices.reshape(8, 2, 2, 2, 4, 2), (*CTX, *TP))
    return jax.shard_map(
        on_device,
        mesh=fine,
        in_specs=(
            P(CTX),
            P(CTX),
            P(),
            P(None, TP),
            P(None, TP),
            P(None, TP),
            P(),
            P(CTX, TP),
            P(CTX, TP),
            P(CTX, TP),
        ),
        out_specs=(P(CTX, TP), P(CTX, TP)),
        check_vma=False,
    )
```

```python
import math

import jax
import jax.numpy as jnp
from jax import lax
from jax.experimental import pallas as pl
from jax.experimental.pallas import tpu as pltpu
from jax.sharding import Mesh
from jax.sharding import PartitionSpec as P

HD = 128
SCALE = math.log2(math.e) / math.sqrt(HD)
NEG = -1e30
N_CTX = 64
N_TP = 8
BYTES_DEV = 512
P_DEV = 128
W_ROWS = 32
VALUES = 128
ROWS = 3 * W_ROWS
MSG = ROWS + 16
PART = P_DEV + 8
VMEM = 20 * 1024 * 1024

Z = ("zh", "zl")
CTX = (*Z, "yl", "c")
PAIR = ("zl", "yl")
TP = ("x", "yh")
PLANES = ("zl", "x", "yh", "yl")
TURN = (*Z, "yl", "x", "yh")


def turned(index, yl):
    return index + yl * (N_TP - 1 - 2 * index)


def flat(z, yl, t):
    return (z * 2 + yl) * N_TP + t


def turns():
    return [
        (flat(z, yl, t), flat(2 * (t ^ 2) + z % 2, yl, turned(z // 2, yl)))
        for z in range(16)
        for yl in range(2)
        for t in range(N_TP)
    ]


def nt_dot(a, b):
    return lax.dot_general(a, b, (((1,), (1,)), ((), ())), preferred_element_type=jnp.float32)


def lens_before(d, c, own_ref, other_ref):
    total = jnp.zeros((), jnp.float32)
    for ref, core in ((own_ref, c), (other_ref, 1 - c)):
        tiles = ref[:, ROWS:, :].astype(jnp.float32)
        slot, row = (lax.broadcasted_iota(jnp.int32, tiles.shape, i) for i in range(2))
        unit, b = slot % 16, slot // 16
        place = 8 * turned(unit // 2, unit % 2) + 4 * b + 2 * (unit % 2) + core
        total = total + jnp.sum(jnp.where((row == 4) & (place < d), tiles, 0.0))
    return total


def byte_counts(d, c, own_ref, other_ref):
    follow = jnp.where(d < N_CTX - 1, d + 1, d - 1)

    def tile(ref, place):
        z, yl = place // 4, (place // 2) % 2
        unit = 2 * turned(z // 2, yl) + yl
        return ref[16 * (z % 2) + unit, ROWS:, :].astype(jnp.float32)

    here, beyond = tile(own_ref, d), tile(other_ref, follow)
    begin = lens_before(d, c, own_ref, other_ref) - (d * BYTES_DEV).astype(jnp.float32)
    lens_row = here[4:5, :]
    row = lax.broadcasted_iota(jnp.int32, (P_DEV, P_DEV), 0)
    col = lax.broadcasted_iota(jnp.int32, (P_DEV, P_DEV), 1)
    lens = jnp.sum(jnp.where(col == row, lens_row, 0.0), axis=1, keepdims=True)
    start = begin + jnp.sum(jnp.where(col < row, lens_row, 0.0), axis=1, keepdims=True)
    end = start + lens
    value = lax.broadcasted_iota(jnp.int32, (256, P_DEV), 0) ^ (VALUES * c)
    value = value.astype(jnp.float32)
    slot = col.astype(jnp.float32)
    counts = jnp.zeros((P_DEV, 256), jnp.float32)
    for chunk in range(6):
        ids = here[chunk : chunk + 1, :] if chunk < 4 else beyond[chunk - 4 : chunk - 3, :]
        at = slot + 128.0 * chunk
        member = ((at >= start) & (at < end)).astype(jnp.bfloat16)
        onehot = (value == ids).astype(jnp.bfloat16)
        counts = counts + nt_dot(member, onehot)
    return counts, lens


def two_heads(counts, lens, table):
    times = counts.astype(jnp.bfloat16)
    share = 1.0 / lens
    hide = jnp.where(counts > 0.0, 0.0, NEG)
    pooled = jnp.dot(times, table[:, :256], preferred_element_type=jnp.float32)
    query = (pooled * share).astype(jnp.bfloat16)
    outs = []
    for a in range(2):
        keys, values = (table[:, (i + a) * HD : (i + a + 1) * HD] for i in (2, 4))
        scores = nt_dot(query[:, a * HD : (a + 1) * HD], keys) * SCALE + hide
        expo = jnp.exp2(scores - jnp.max(scores, axis=-1, keepdims=True))
        norm = jnp.sum(expo * counts, axis=-1, keepdims=True)
        weights = (expo * (1.0 / norm)).astype(jnp.bfloat16) * times
        out = jnp.dot(weights, values, preferred_element_type=jnp.float32)
        outs.append(out.astype(jnp.bfloat16))
    return jnp.concatenate(outs, axis=1)


def coordinates():
    zh, zl, yl, c = (lax.axis_index(name) for name in CTX)
    return 2 * zh + zl, yl, c, 2 * lax.axis_index("x") + lax.axis_index("yh")


def table_of(tt, refs):
    return jnp.concatenate([ref[tt] for ref in refs], axis=0)


def start_kernel(
    ids_ref, lens_ref, table_ref, wq, wk, wv, lq, lk, lv, tables_ref, message_ref
):
    _, _, c, _ = coordinates()
    first = pl.multiple_of(VALUES * c, VALUES)
    rows = table_ref[pl.ds(first, VALUES), :]
    for i, ref in enumerate((wq, wk, wv)):
        part = jnp.dot(rows, ref[...], preferred_element_type=jnp.float32).astype(jnp.bfloat16)
        for tt in range(N_TP):
            tables_ref[tt, :, 2 * i * HD : 2 * (i + 1) * HD] = part
    ints = jnp.concatenate(
        [ids_ref[...], lens_ref[...], jnp.zeros((11, HD), jnp.int32)], axis=0
    ).astype(jnp.float32)
    for a in range(2):
        for i, ref in enumerate((lq, lk, lv)):
            message_ref[a, i * W_ROWS : (i + 1) * W_ROWS, :] = ref[:, a * HD : (a + 1) * HD]
        message_ref[a, ROWS:, :] = ints.astype(jnp.bfloat16)


def encode_kernel(*refs):
    tables = refs[:2]
    own_ref, other_ref, gain_ref, q_ref, kv_ref, latent, weight = refs[2:]
    _, yl, c, t = coordinates()
    first_z = 2 * turned(t, yl)
    parts = [
        byte_counts(4 * z + 2 * yl + c, c, own_ref, other_ref)
        for z in (first_z, first_z + 1)
    ]
    counts = jnp.concatenate([part[0] for part in parts], axis=0)
    lens = jnp.concatenate([part[1] for part in parts], axis=0)

    def heads(tt, squares):
        out = two_heads(counts, lens, table_of(tt, tables))
        latent[tt] = out
        wide = out.astype(jnp.float32)
        for ref, core in ((own_ref, c), (other_ref, 1 - c)):
            for b in range(2):
                for side in range(2):
                    first = pl.multiple_of(W_ROWS * (4 * b + 2 * side + core), W_ROWS)
                    for n in range(3):
                        weight[turned(tt, side), pl.ds(first, W_ROWS), n * HD : (n + 1) * HD] = ref[
                            16 * b + 2 * tt + side, n * W_ROWS : (n + 1) * W_ROWS, :
                        ]
        return squares + jnp.sum(wide * wide, axis=-1, keepdims=True)

    squares = lax.fori_loop(0, N_TP, heads, jnp.zeros((2 * P_DEV, 1), jnp.float32), unroll=8)
    inverse = lax.rsqrt(squares / 2048.0 + 1e-05)
    total = jnp.zeros((2 * P_DEV, 3 * HD), jnp.float32)
    for tt in range(N_TP):
        gain = gain_ref[:, tt * 256 : (tt + 1) * 256]
        normed = latent[tt].astype(jnp.float32) * inverse * gain
        total = total + jnp.dot(
            normed.astype(jnp.bfloat16), weight[tt], preferred_element_type=jnp.float32
        )
    total = total.astype(jnp.bfloat16)
    q_ref[...] = total[:, :HD]
    for tt in range(N_TP):
        kv_ref[tt] = total[:, HD:]


def latent_kernel(*refs):
    own_ref, other_ref, out_ref = refs[2:]
    z, yl, c, t = coordinates()
    counts, lens = byte_counts(4 * z + 2 * yl + c, c, own_ref, other_ref)
    out_ref[...] = two_heads(counts, lens, table_of(t, refs[:2]))


def diagonal():
    shape = (P_DEV, P_DEV)
    return lax.broadcasted_iota(jnp.int32, shape, 0) == lax.broadcasted_iota(jnp.int32, shape, 1)


def as_row(column):
    return jnp.sum(jnp.where(diagonal(), column, 0.0), axis=0, keepdims=True)


def as_column(row):
    return jnp.sum(jnp.where(diagonal(), row, 0.0), axis=1, keepdims=True)


def attend_kernel(
    q_own,
    q_other,
    kv_own,
    kv_other,
    out_ref,
    scores,
    query,
    tops,
    norms,
    accs,
):
    _, yl, c, t = coordinates()
    size = 2 * P_DEV
    query[yl] = q_own[...]
    query[1 - yl] = q_other[...]
    tops[...] = jnp.full(tops.shape, NEG, jnp.float32)
    norms[...] = jnp.zeros(norms.shape, jnp.float32)
    accs[...] = jnp.zeros(accs.shape, jnp.float32)
    row = lax.broadcasted_iota(jnp.int32, (size, size), 0)
    col = lax.broadcasted_iota(jnp.int32, (size, size), 1)
    behind = 512 * (row // P_DEV - col // P_DEV) + row % P_DEV - col % P_DEV

    def hide(q_yl, core):
        return jnp.where(behind + 256 * (q_yl - yl) + P_DEV * (c - core) >= 0, 0.0, NEG)

    units = N_TP + 1

    def unit(u):
        if u == N_TP:
            return 1, turned(N_TP - 1 - t, yl)
        first = u <= t
        return jnp.where(first, 0, 1), turned(jnp.where(first, u, u - t - 1), yl)

    sides = ((kv_own, c), (kv_other, 1 - c))
    for u in range(units):
        q_yl, tt = unit(u)
        best = tops[q_yl]
        for i, (ref, core) in enumerate(sides):
            s = nt_dot(query[q_yl], ref[tt, :, :HD]) * SCALE
            if u == N_TP:
                s = s + hide(1, core)
            else:
                s = s + hide(0, core) * jnp.where(u == t, 1.0, 0.0)
            scores[u, i] = s
            best = jnp.maximum(best, jnp.maximum(s[:, :HD], s[:, HD:]))
        tops[q_yl] = best
    for b in range(2):
        tops[b] = jnp.broadcast_to(jnp.max(tops[b], axis=-1, keepdims=True), (size, HD))
    for u in range(units):
        q_yl, tt = unit(u)
        top = tops[q_yl]
        top = jnp.concatenate([top, top], axis=1)
        norm, acc = norms[q_yl], accs[q_yl]
        for i, (ref, _) in enumerate(sides):
            e = jnp.exp2(scores[u, i] - top)
            norm = norm + (e[:, :HD] + e[:, HD:])
            acc = acc + jnp.dot(
                e.astype(jnp.bfloat16), ref[tt, :, HD:], preferred_element_type=jnp.float32
            )
        norms[q_yl] = norm
        accs[q_yl] = acc
    for b in range(2):
        rows = slice(b * P_DEV, (b + 1) * P_DEV)
        for q_yl in range(2):
            slot = 2 * b + q_yl
            out_ref[slot, :P_DEV, :] = accs[q_yl, rows, :]
            total = jnp.sum(norms[q_yl, rows, :], axis=-1, keepdims=True)
            stats = [as_row(tops[q_yl, rows, :1]), as_row(total), jnp.zeros((6, HD), jnp.float32)]
            out_ref[slot, P_DEV:, :] = jnp.concatenate(stats, axis=0)


def join_kernel(part_ref, out_ref):
    for a in range(2):
        slots = (2 * a, 2 * a + 1)
        tops = [as_column(part_ref[i, P_DEV : P_DEV + 1, :]) for i in slots]
        sums = [as_column(part_ref[i, P_DEV + 1 : P_DEV + 2, :]) for i in slots]
        top = jnp.maximum(*tops)
        scale = [jnp.exp2(part - top) for part in tops]
        mixed = part_ref[slots[0], :P_DEV, :] * scale[0] + part_ref[slots[1], :P_DEV, :] * scale[1]
        mixed = mixed / (sums[0] * scale[0] + sums[1] * scale[1])
        out_ref[:, a * HD : (a + 1) * HD] = mixed.astype(jnp.bfloat16)


def call(body, outs, scratch, flops, *args, limit=VMEM):
    vmem = pl.BlockSpec(memory_space=pltpu.VMEM)
    return pl.pallas_call(
        body,
        out_shape=[jax.ShapeDtypeStruct(shape, dtype) for shape, dtype in outs],
        in_specs=[vmem] * len(args),
        out_specs=[vmem] * len(outs),
        scratch_shapes=[pltpu.VMEM(shape, dtype) for shape, dtype in scratch],
        compiler_params=pltpu.CompilerParams(vmem_limit_bytes=limit),
        cost_estimate=pl.CostEstimate(flops=flops, bytes_accessed=4 << 20, transcendentals=1 << 20),
    )(*args)


BF, F32 = jnp.bfloat16, jnp.float32


def run_start(*args):
    outs = [((N_TP, VALUES, 6 * HD), BF), ((2, MSG, HD), BF)]
    return call(start_kernel, outs, [], 1 << 28, *args, limit=56 << 20)


def run_encode(*args):
    outs = [((2 * P_DEV, HD), BF), ((N_TP, 2 * P_DEV, 2 * HD), BF)]
    scratch = [((N_TP, 256, 256), BF), ((N_TP, 256, 3 * HD), BF)]
    return call(encode_kernel, outs, scratch, 1 << 30, *args)


def run_latent(*args):
    return call(latent_kernel, [((P_DEV, 256), BF)], [], 1 << 26, *args)[0]


def run_attend(*args):
    size = 2 * P_DEV
    block = (2, size, HD)
    scratch = [((N_TP + 1, 2, size, size), F32), (block, BF)] + [(block, F32)] * 3
    return call(attend_kernel, [((4, PART, HD), F32)], scratch, 1 << 30, *args)[0]


def run_join(*args):
    return call(join_kernel, [((P_DEV, 2 * HD), BF)], [], 1 << 20, *args)[0]


def on_device(
    byte_ids,
    patch_lens,
    byte_table,
    wq_cross,
    wk_cross,
    wv_cross,
    norm_gain,
    wq_latent,
    wk_latent,
    wv_latent,
):
    swap = [(0, 1), (1, 0)]
    turn = turns()

    tables, message = run_start(
        byte_ids.reshape(4, HD),
        patch_lens.reshape(1, HD),
        byte_table,
        wq_cross,
        wk_cross,
        wv_cross,
        wq_latent,
        wk_latent,
        wv_latent,
    )
    message = lax.ppermute(message, TURN, turn)
    tab_own = lax.all_to_all(tables, TP, 0, 0)
    byte_tables = (tab_own, lax.ppermute(tab_own, "c", swap))
    message = jnp.broadcast_to(message[:, None], (2, 16, MSG, HD)).reshape(32, MSG, HD)
    msg_own = lax.all_to_all(message, PLANES, 0, 0, tiled=True)
    msg_other = lax.ppermute(msg_own, "c", swap)

    q, kv = run_encode(*byte_tables, msg_own, msg_other, norm_gain.reshape(1, 2048))
    q_other = lax.ppermute(q, "yl", swap)
    kv_own = lax.all_to_all(kv, TP, 0, 0)
    patch_latent = run_latent(*byte_tables, msg_own, msg_other)
    kv_own, q_other, patch_latent = lax.optimization_barrier((kv_own, q_other, patch_latent))
    kv_other = lax.ppermute(kv_own, "c", swap)
    parts = run_attend(q, q_other, kv_own, kv_other)
    mixed = run_join(lax.all_to_all(parts, PAIR, 0, 0))
    latent_mixed = lax.ppermute(mixed, TURN, [(target, source) for source, target in turn])
    return (patch_latent, latent_mixed)


def solution(mesh):
    fine = Mesh(mesh.devices.reshape(8, 2, 2, 2, 4, 2), (*CTX, *TP))
    return jax.shard_map(
        on_device,
        mesh=fine,
        in_specs=(
            P(CTX),
            P(CTX),
            P(),
            P(None, TP),
            P(None, TP),
            P(None, TP),
            P(),
            P(CTX, TP),
            P(CTX, TP),
            P(CTX, TP),
        ),
        out_specs=(P(CTX, TP), P(CTX, TP)),
        check_vma=False,
    )
```

```python
import math

import jax
import jax.numpy as jnp
from jax import lax
from jax.experimental import pallas as pl
from jax.experimental.pallas import tpu as pltpu
from jax.sharding import Mesh
from jax.sharding import PartitionSpec as P

HD = 128
SCALE = math.log2(math.e) / math.sqrt(HD)
NEG = -1e30
N_CTX = 64
N_TP = 8
BYTES_DEV = 512
P_DEV = 128
W_ROWS = 32
VALUES = 128
ROWS = 3 * W_ROWS
MSG = ROWS + 16
PART = P_DEV + 16
VMEM = 20 * 1024 * 1024

Z = ("zh", "zl")
CTX = (*Z, "yl", "c")
PAIR = ("zl", "yl")
TP = ("x", "yh")
PLANES = ("zl", "x", "yh", "yl")
TURN = (*Z, "yl", "x", "yh")


def turned(index, yl):
    return index + yl * (N_TP - 1 - 2 * index)


def flat(z, yl, t):
    return (z * 2 + yl) * N_TP + t


def turns():
    return [
        (flat(z, yl, t), flat(2 * (t ^ 2) + z % 2, yl, turned(z // 2, yl)))
        for z in range(16)
        for yl in range(2)
        for t in range(N_TP)
    ]


def nt_dot(a, b):
    return lax.dot_general(a, b, (((1,), (1,)), ((), ())), preferred_element_type=jnp.float32)


def lens_before(d, c, own_ref, other_ref):
    total = jnp.zeros((), jnp.float32)
    for ref, core in ((own_ref, c), (other_ref, 1 - c)):
        tiles = ref[:, ROWS:, :].astype(jnp.float32)
        slot, row = (lax.broadcasted_iota(jnp.int32, tiles.shape, i) for i in range(2))
        unit, b = slot % 16, slot // 16
        place = 8 * turned(unit // 2, unit % 2) + 4 * b + 2 * (unit % 2) + core
        total = total + jnp.sum(jnp.where((row == 4) & (place < d), tiles, 0.0))
    return total


def byte_counts(d, c, own_ref, other_ref):
    follow = jnp.where(d < N_CTX - 1, d + 1, d - 1)

    def tile(ref, place):
        z, yl = place // 4, (place // 2) % 2
        unit = 2 * turned(z // 2, yl) + yl
        return ref[16 * (z % 2) + unit, ROWS:, :].astype(jnp.float32)

    here, beyond = tile(own_ref, d), tile(other_ref, follow)
    begin = lens_before(d, c, own_ref, other_ref) - (d * BYTES_DEV).astype(jnp.float32)
    lens_row = here[4:5, :]
    row = lax.broadcasted_iota(jnp.int32, (P_DEV, P_DEV), 0)
    col = lax.broadcasted_iota(jnp.int32, (P_DEV, P_DEV), 1)
    lens = jnp.sum(jnp.where(col == row, lens_row, 0.0), axis=1, keepdims=True)
    start = begin + jnp.sum(jnp.where(col < row, lens_row, 0.0), axis=1, keepdims=True)
    end = start + lens
    value = lax.broadcasted_iota(jnp.int32, (256, P_DEV), 0) ^ (VALUES * c)
    value = value.astype(jnp.float32)
    slot = col.astype(jnp.float32)
    counts = jnp.zeros((P_DEV, 256), jnp.float32)
    for chunk in range(6):
        ids = here[chunk : chunk + 1, :] if chunk < 4 else beyond[chunk - 4 : chunk - 3, :]
        at = slot + 128.0 * chunk
        member = ((at >= start) & (at < end)).astype(jnp.bfloat16)
        onehot = (value == ids).astype(jnp.bfloat16)
        counts = counts + nt_dot(member, onehot)
    return counts, lens


def two_heads(counts, lens, table):
    times = counts.astype(jnp.bfloat16)
    share = 1.0 / lens
    hide = jnp.where(counts > 0.0, 0.0, NEG)
    pooled = jnp.dot(times, table[:, :256], preferred_element_type=jnp.float32)
    query = (pooled * share).astype(jnp.bfloat16)
    outs = []
    for a in range(2):
        keys, values = (table[:, (i + a) * HD : (i + a + 1) * HD] for i in (2, 4))
        scores = nt_dot(query[:, a * HD : (a + 1) * HD], keys) * SCALE + hide
        expo = jnp.exp2(scores - jnp.max(scores, axis=-1, keepdims=True))
        norm = jnp.sum(expo * counts, axis=-1, keepdims=True)
        weights = (expo * (1.0 / norm)).astype(jnp.bfloat16) * times
        out = jnp.dot(weights, values, preferred_element_type=jnp.float32)
        outs.append(out.astype(jnp.bfloat16))
    return jnp.concatenate(outs, axis=1)


def coordinates():
    zh, zl, yl, c = (lax.axis_index(name) for name in CTX)
    return 2 * zh + zl, yl, c, 2 * lax.axis_index("x") + lax.axis_index("yh")


def table_of(tt, refs):
    return jnp.concatenate([ref[tt] for ref in refs], axis=0)


def start_kernel(
    ids_ref, lens_ref, table_ref, wq, wk, wv, lq, lk, lv, tables_ref, message_ref
):
    _, _, c, _ = coordinates()
    first = pl.multiple_of(VALUES * c, VALUES)
    rows = table_ref[pl.ds(first, VALUES), :]
    for i, ref in enumerate((wq, wk, wv)):
        part = jnp.dot(rows, ref[...], preferred_element_type=jnp.float32).astype(jnp.bfloat16)
        for tt in range(N_TP):
            tables_ref[tt, :, 2 * i * HD : 2 * (i + 1) * HD] = part
    ints = jnp.concatenate(
        [ids_ref[...], lens_ref[...], jnp.zeros((11, HD), jnp.int32)], axis=0
    ).astype(jnp.float32)
    for a in range(2):
        for i, ref in enumerate((lq, lk, lv)):
            message_ref[a, i * W_ROWS : (i + 1) * W_ROWS, :] = ref[:, a * HD : (a + 1) * HD]
        message_ref[a, ROWS:, :] = ints.astype(jnp.bfloat16)


def encode_kernel(*refs):
    tables = refs[:2]
    own_ref, other_ref, gain_ref, q_ref, kv_ref, latent, weight = refs[2:]
    _, yl, c, t = coordinates()
    first_z = 2 * turned(t, yl)
    parts = [
        byte_counts(4 * z + 2 * yl + c, c, own_ref, other_ref)
        for z in (first_z, first_z + 1)
    ]
    counts = jnp.concatenate([part[0] for part in parts], axis=0)
    lens = jnp.concatenate([part[1] for part in parts], axis=0)

    def heads(tt, squares):
        out = two_heads(counts, lens, table_of(tt, tables))
        latent[tt] = out
        wide = out.astype(jnp.float32)
        for ref, core in ((own_ref, c), (other_ref, 1 - c)):
            for b in range(2):
                for side in range(2):
                    first = pl.multiple_of(W_ROWS * (4 * b + 2 * side + core), W_ROWS)
                    for n in range(3):
                        weight[turned(tt, side), pl.ds(first, W_ROWS), n * HD : (n + 1) * HD] = ref[
                            16 * b + 2 * tt + side, n * W_ROWS : (n + 1) * W_ROWS, :
                        ]
        return squares + jnp.sum(wide * wide, axis=-1, keepdims=True)

    squares = lax.fori_loop(0, N_TP, heads, jnp.zeros((2 * P_DEV, 1), jnp.float32), unroll=8)
    inverse = lax.rsqrt(squares / 2048.0 + 1e-05)
    total = jnp.zeros((2 * P_DEV, 3 * HD), jnp.float32)
    for tt in range(N_TP):
        gain = gain_ref[:, tt * 256 : (tt + 1) * 256]
        normed = latent[tt].astype(jnp.float32) * inverse * gain
        total = total + jnp.dot(
            normed.astype(jnp.bfloat16), weight[tt], preferred_element_type=jnp.float32
        )
    total = total.astype(jnp.bfloat16)
    q_ref[...] = total[:, :HD]
    for tt in range(N_TP):
        kv_ref[tt] = total[:, HD:]


def latent_kernel(*refs):
    own_ref, other_ref, out_ref = refs[2:]
    z, yl, c, t = coordinates()
    counts, lens = byte_counts(4 * z + 2 * yl + c, c, own_ref, other_ref)
    out_ref[...] = two_heads(counts, lens, table_of(t, refs[:2]))


def diagonal():
    shape = (P_DEV, P_DEV)
    return lax.broadcasted_iota(jnp.int32, shape, 0) == lax.broadcasted_iota(jnp.int32, shape, 1)


def as_row(column):
    return jnp.sum(jnp.where(diagonal(), column, 0.0), axis=0, keepdims=True)


def as_column(row):
    return jnp.sum(jnp.where(diagonal(), row, 0.0), axis=1, keepdims=True)


def attend_kernel(
    q_own,
    q_other,
    kv_own,
    kv_other,
    out_ref,
    scores,
    query,
    tops,
    norms,
    accs,
):
    _, yl, c, t = coordinates()
    size = 2 * P_DEV
    query[yl] = q_own[...]
    query[1 - yl] = q_other[...]
    tops[...] = jnp.full(tops.shape, NEG, jnp.float32)
    norms[...] = jnp.zeros(norms.shape, jnp.float32)
    accs[...] = jnp.zeros(accs.shape, jnp.float32)
    row = lax.broadcasted_iota(jnp.int32, (size, size), 0)
    col = lax.broadcasted_iota(jnp.int32, (size, size), 1)
    behind = 512 * (row // P_DEV - col // P_DEV) + row % P_DEV - col % P_DEV

    def hide(q_yl, core):
        return jnp.where(behind + 256 * (q_yl - yl) + P_DEV * (c - core) >= 0, 0.0, NEG)

    units = N_TP + 1

    def unit(u):
        if u == N_TP:
            return 1, turned(N_TP - 1 - t, yl)
        first = u <= t
        return jnp.where(first, 0, 1), turned(jnp.where(first, u, u - t - 1), yl)

    sides = ((kv_own, c), (kv_other, 1 - c))
    for u in range(units):
        q_yl, tt = unit(u)
        best = tops[q_yl]
        for i, (ref, core) in enumerate(sides):
            s = nt_dot(query[q_yl], ref[tt, :, :HD]) * SCALE
            if u == N_TP:
                s = s + hide(1, core)
            else:
                s = s + hide(0, core) * jnp.where(u == t, 1.0, 0.0)
            scores[u, i] = s
            best = jnp.maximum(best, jnp.maximum(s[:, :HD], s[:, HD:]))
        tops[q_yl] = best
    for b in range(2):
        tops[b] = jnp.broadcast_to(jnp.max(tops[b], axis=-1, keepdims=True), (size, HD))
    for u in range(units):
        q_yl, tt = unit(u)
        top = tops[q_yl]
        top = jnp.concatenate([top, top], axis=1)
        norm, acc = norms[q_yl], accs[q_yl]
        for i, (ref, _) in enumerate(sides):
            e = jnp.exp2(scores[u, i] - top)
            norm = norm + (e[:, :HD] + e[:, HD:])
            acc = acc + jnp.dot(
                e.astype(jnp.bfloat16), ref[tt, :, HD:], preferred_element_type=jnp.float32
            )
        norms[q_yl] = norm
        accs[q_yl] = acc
    for b in range(2):
        rows = slice(b * P_DEV, (b + 1) * P_DEV)
        for q_yl in range(2):
            slot = 2 * b + q_yl
            total = jnp.sum(norms[q_yl, rows, :], axis=-1, keepdims=True)
            out_ref[slot, :P_DEV, :] = (accs[q_yl, rows, :] / total).astype(jnp.bfloat16)
            rest = as_row(tops[q_yl, rows, :1] + jnp.log2(total))
            pieces = []
            for _ in range(3):
                pieces.append(rest.astype(jnp.bfloat16).astype(jnp.float32))
                rest = rest - pieces[-1]
            pieces.append(jnp.zeros((13, HD), jnp.float32))
            out_ref[slot, P_DEV:, :] = jnp.concatenate(pieces, axis=0).astype(jnp.bfloat16)


def join_kernel(part_ref, out_ref):
    for a in range(2):
        parts, logs = [], []
        for i in (2 * a, 2 * a + 1):
            parts.append(part_ref[i, :P_DEV, :].astype(jnp.float32))
            tail = part_ref[i, P_DEV:, :].astype(jnp.float32)
            logs.append(as_column(tail[0:1, :] + tail[1:2, :] + tail[2:3, :]))
        top = jnp.maximum(*logs)
        scale = [jnp.exp2(log - top) for log in logs]
        mixed = (parts[0] * scale[0] + parts[1] * scale[1]) / (scale[0] + scale[1])
        out_ref[:, a * HD : (a + 1) * HD] = mixed.astype(jnp.bfloat16)


def call(body, outs, scratch, flops, *args, limit=VMEM):
    vmem = pl.BlockSpec(memory_space=pltpu.VMEM)
    return pl.pallas_call(
        body,
        out_shape=[jax.ShapeDtypeStruct(shape, dtype) for shape, dtype in outs],
        in_specs=[vmem] * len(args),
        out_specs=[vmem] * len(outs),
        scratch_shapes=[pltpu.VMEM(shape, dtype) for shape, dtype in scratch],
        compiler_params=pltpu.CompilerParams(vmem_limit_bytes=limit),
        cost_estimate=pl.CostEstimate(flops=flops, bytes_accessed=4 << 20, transcendentals=1 << 20),
    )(*args)


BF, F32 = jnp.bfloat16, jnp.float32


def run_start(*args):
    outs = [((N_TP, VALUES, 6 * HD), BF), ((2, MSG, HD), BF)]
    return call(start_kernel, outs, [], 1 << 28, *args, limit=56 << 20)


def run_encode(*args):
    outs = [((2 * P_DEV, HD), BF), ((N_TP, 2 * P_DEV, 2 * HD), BF)]
    scratch = [((N_TP, 256, 256), BF), ((N_TP, 256, 3 * HD), BF)]
    return call(encode_kernel, outs, scratch, 1 << 30, *args)


def run_latent(*args):
    return call(latent_kernel, [((P_DEV, 256), BF)], [], 1 << 26, *args)[0]


def run_attend(*args):
    size = 2 * P_DEV
    block = (2, size, HD)
    scratch = [((N_TP + 1, 2, size, size), F32), (block, BF)] + [(block, F32)] * 3
    return call(attend_kernel, [((4, PART, HD), BF)], scratch, 1 << 30, *args)[0]


def run_join(*args):
    return call(join_kernel, [((P_DEV, 2 * HD), BF)], [], 1 << 20, *args)[0]


def on_device(
    byte_ids,
    patch_lens,
    byte_table,
    wq_cross,
    wk_cross,
    wv_cross,
    norm_gain,
    wq_latent,
    wk_latent,
    wv_latent,
):
    swap = [(0, 1), (1, 0)]
    turn = turns()

    tables, message = run_start(
        byte_ids.reshape(4, HD),
        patch_lens.reshape(1, HD),
        byte_table,
        wq_cross,
        wk_cross,
        wv_cross,
        wq_latent,
        wk_latent,
        wv_latent,
    )
    message = lax.ppermute(message, TURN, turn)
    tab_own = lax.all_to_all(tables, TP, 0, 0)
    byte_tables = (tab_own, lax.ppermute(tab_own, "c", swap))
    message = jnp.broadcast_to(message[:, None], (2, 16, MSG, HD)).reshape(32, MSG, HD)
    msg_own = lax.all_to_all(message, PLANES, 0, 0, tiled=True)
    msg_other = lax.ppermute(msg_own, "c", swap)

    q, kv = run_encode(*byte_tables, msg_own, msg_other, norm_gain.reshape(1, 2048))
    q_other = lax.ppermute(q, "yl", swap)
    kv_own = lax.all_to_all(kv, TP, 0, 0)
    patch_latent = run_latent(*byte_tables, msg_own, msg_other)
    kv_own, q_other, patch_latent = lax.optimization_barrier((kv_own, q_other, patch_latent))
    kv_other = lax.ppermute(kv_own, "c", swap)
    parts = run_attend(q, q_other, kv_own, kv_other)
    mixed = run_join(lax.all_to_all(parts, PAIR, 0, 0))
    latent_mixed = lax.ppermute(mixed, TURN, [(target, source) for source, target in turn])
    return (patch_latent, latent_mixed)


def solution(mesh):
    fine = Mesh(mesh.devices.reshape(8, 2, 2, 2, 4, 2), (*CTX, *TP))
    return jax.shard_map(
        on_device,
        mesh=fine,
        in_specs=(
            P(CTX),
            P(CTX),
            P(),
            P(None, TP),
            P(None, TP),
            P(None, TP),
            P(),
            P(CTX, TP),
            P(CTX, TP),
            P(CTX, TP),
        ),
        out_specs=(P(CTX, TP), P(CTX, TP)),
        check_vma=False,
    )
```

```python
import functools
import math

import jax
import jax.numpy as jnp
from jax import lax
from jax.experimental import pallas as pl
from jax.experimental.pallas import tpu as pltpu
from jax.sharding import Mesh
from jax.sharding import PartitionSpec as P

HD = 128
SCALE = math.log2(math.e) / math.sqrt(HD)
NEG = -1e30
N_CTX = 64
N_TP = 8
BYTES_DEV = 512
P_DEV = 128
W_ROWS = 32
VALUES = 128
ROWS = 3 * W_ROWS
MSG = ROWS + 16
PART = P_DEV + 16
VMEM = 20 * 1024 * 1024

Z = ("zh", "zl")
CTX = (*Z, "yl", "c")
PAIR = ("zl", "yl")
TP = ("x", "yh")
PLANES = ("zl", "x", "yh", "yl")
TURN = (*Z, "yl", "x", "yh")


def turned(index, yl):
    return index + yl * (N_TP - 1 - 2 * index)


def flat(z, yl, t):
    return (z * 2 + yl) * N_TP + t


def turns():
    return [
        (flat(z, yl, t), flat(2 * (t ^ 2) + z % 2, yl, turned(z // 2, yl)))
        for z in range(16)
        for yl in range(2)
        for t in range(N_TP)
    ]


def nt_dot(a, b):
    return lax.dot_general(a, b, (((1,), (1,)), ((), ())), preferred_element_type=jnp.float32)


def lens_before(d, c, own_ref, other_ref):
    total = jnp.zeros((), jnp.float32)
    for ref, core in ((own_ref, c), (other_ref, 1 - c)):
        tiles = ref[:, ROWS:, :].astype(jnp.float32)
        slot, row = (lax.broadcasted_iota(jnp.int32, tiles.shape, i) for i in range(2))
        unit, b = slot % 16, slot // 16
        place = 8 * turned(unit // 2, unit % 2) + 4 * b + 2 * (unit % 2) + core
        total = total + jnp.sum(jnp.where((row == 4) & (place < d), tiles, 0.0))
    return total


def byte_counts(d, c, own_ref, other_ref):
    follow = jnp.where(d < N_CTX - 1, d + 1, d - 1)

    def tile(ref, place):
        z, yl = place // 4, (place // 2) % 2
        unit = 2 * turned(z // 2, yl) + yl
        return ref[16 * (z % 2) + unit, ROWS:, :].astype(jnp.float32)

    here, beyond = tile(own_ref, d), tile(other_ref, follow)
    begin = lens_before(d, c, own_ref, other_ref) - (d * BYTES_DEV).astype(jnp.float32)
    lens_row = here[4:5, :]
    row = lax.broadcasted_iota(jnp.int32, (P_DEV, P_DEV), 0)
    col = lax.broadcasted_iota(jnp.int32, (P_DEV, P_DEV), 1)
    lens = jnp.sum(jnp.where(col == row, lens_row, 0.0), axis=1, keepdims=True)
    start = begin + jnp.sum(jnp.where(col < row, lens_row, 0.0), axis=1, keepdims=True)
    end = start + lens
    value = lax.broadcasted_iota(jnp.int32, (256, P_DEV), 0) ^ (VALUES * c)
    value = value.astype(jnp.float32)
    slot = col.astype(jnp.float32)
    counts = jnp.zeros((P_DEV, 256), jnp.float32)
    for chunk in range(6):
        ids = here[chunk : chunk + 1, :] if chunk < 4 else beyond[chunk - 4 : chunk - 3, :]
        at = slot + 128.0 * chunk
        member = ((at >= start) & (at < end)).astype(jnp.bfloat16)
        onehot = (value == ids).astype(jnp.bfloat16)
        counts = counts + nt_dot(member, onehot)
    return counts, lens


def two_heads(counts, lens, table):
    times = counts.astype(jnp.bfloat16)
    share = 1.0 / lens
    hide = jnp.where(counts > 0.0, 0.0, NEG)
    pooled = jnp.dot(times, table[:, :256], preferred_element_type=jnp.float32)
    query = (pooled * share).astype(jnp.bfloat16)
    outs = []
    for a in range(2):
        keys, values = (table[:, (i + a) * HD : (i + a + 1) * HD] for i in (2, 4))
        scores = nt_dot(query[:, a * HD : (a + 1) * HD], keys) * SCALE + hide
        expo = jnp.exp2(scores - jnp.max(scores, axis=-1, keepdims=True))
        norm = jnp.sum(expo * counts, axis=-1, keepdims=True)
        weights = (expo * (1.0 / norm)).astype(jnp.bfloat16) * times
        out = jnp.dot(weights, values, preferred_element_type=jnp.float32)
        outs.append(out.astype(jnp.bfloat16))
    return jnp.concatenate(outs, axis=1)


def coordinates():
    zh, zl, yl, c = (lax.axis_index(name) for name in CTX)
    return 2 * zh + zl, yl, c, 2 * lax.axis_index("x") + lax.axis_index("yh")


def table_of(tt, refs):
    return jnp.concatenate([ref[tt] for ref in refs], axis=0)


def start_kernel(
    ids_ref, lens_ref, table_ref, wq, wk, wv, lq, lk, lv, tables_ref, message_ref
):
    _, _, c, _ = coordinates()
    first = pl.multiple_of(VALUES * c, VALUES)
    rows = table_ref[pl.ds(first, VALUES), :]
    for i, ref in enumerate((wq, wk, wv)):
        part = jnp.dot(rows, ref[...], preferred_element_type=jnp.float32).astype(jnp.bfloat16)
        for tt in range(N_TP):
            tables_ref[tt, :, 2 * i * HD : 2 * (i + 1) * HD] = part
    ints = jnp.concatenate(
        [ids_ref[...], lens_ref[...], jnp.zeros((11, HD), jnp.int32)], axis=0
    ).astype(jnp.float32)
    for a in range(2):
        for i, ref in enumerate((lq, lk, lv)):
            message_ref[a, i * W_ROWS : (i + 1) * W_ROWS, :] = ref[:, a * HD : (a + 1) * HD]
        message_ref[a, ROWS:, :] = ints.astype(jnp.bfloat16)


def encode_kernel(*refs):
    tables = refs[:2]
    own_ref, other_ref, gain_ref, q_ref, kv_ref, latent, weight = refs[2:]
    _, yl, c, t = coordinates()
    first_z = 2 * turned(t, yl)
    parts = [
        byte_counts(4 * z + 2 * yl + c, c, own_ref, other_ref)
        for z in (first_z, first_z + 1)
    ]
    counts = jnp.concatenate([part[0] for part in parts], axis=0)
    lens = jnp.concatenate([part[1] for part in parts], axis=0)

    def heads(tt, squares):
        out = two_heads(counts, lens, table_of(tt, tables))
        latent[tt] = out
        wide = out.astype(jnp.float32)
        for ref, core in ((own_ref, c), (other_ref, 1 - c)):
            for b in range(2):
                for side in range(2):
                    first = pl.multiple_of(W_ROWS * (4 * b + 2 * side + core), W_ROWS)
                    for n in range(3):
                        weight[turned(tt, side), pl.ds(first, W_ROWS), n * HD : (n + 1) * HD] = ref[
                            16 * b + 2 * tt + side, n * W_ROWS : (n + 1) * W_ROWS, :
                        ]
        return squares + jnp.sum(wide * wide, axis=-1, keepdims=True)

    squares = lax.fori_loop(0, N_TP, heads, jnp.zeros((2 * P_DEV, 1), jnp.float32), unroll=8)
    inverse = lax.rsqrt(squares / 2048.0 + 1e-05)
    total = jnp.zeros((2 * P_DEV, 3 * HD), jnp.float32)
    for tt in range(N_TP):
        gain = gain_ref[:, tt * 256 : (tt + 1) * 256]
        normed = latent[tt].astype(jnp.float32) * inverse * gain
        total = total + jnp.dot(
            normed.astype(jnp.bfloat16), weight[tt], preferred_element_type=jnp.float32
        )
    total = total.astype(jnp.bfloat16)
    q_ref[...] = total[:, :HD]
    for tt in range(N_TP):
        kv_ref[tt] = total[:, HD:]


def latent_kernel(*refs):
    own_ref, other_ref, out_ref = refs[2:]
    z, yl, c, t = coordinates()
    counts, lens = byte_counts(4 * z + 2 * yl + c, c, own_ref, other_ref)
    out_ref[...] = two_heads(counts, lens, table_of(t, refs[:2]))


def diagonal():
    shape = (P_DEV, P_DEV)
    return lax.broadcasted_iota(jnp.int32, shape, 0) == lax.broadcasted_iota(jnp.int32, shape, 1)


def as_row(column):
    return jnp.sum(jnp.where(diagonal(), column, 0.0), axis=0, keepdims=True)


def as_column(row):
    return jnp.sum(jnp.where(diagonal(), row, 0.0), axis=1, keepdims=True)


def attend_kernel(last, *refs):
    q_own, q_other, kv_ref = refs[:3]
    if last:
        top_in, norm_in, acc_in, out_ref, scores, query, tops, norms, accs = refs[3:]
    else:
        tops, norms, accs, scores, query = refs[3:]
    _, yl, c, t = coordinates()
    size = 2 * P_DEV
    query[yl] = q_own[...]
    query[1 - yl] = q_other[...]
    tops[...] = top_in[...] if last else jnp.full(tops.shape, NEG, jnp.float32)
    row = lax.broadcasted_iota(jnp.int32, (size, size), 0)
    col = lax.broadcasted_iota(jnp.int32, (size, size), 1)
    behind = 512 * (row // P_DEV - col // P_DEV) + row % P_DEV - col % P_DEV

    def hide(q_yl, core):
        return jnp.where(behind + 256 * (q_yl - yl) + P_DEV * (c - core) >= 0, 0.0, NEG)

    units = N_TP + 1

    def unit(u):
        if u == N_TP:
            return 1, turned(N_TP - 1 - t, yl)
        first = u <= t
        return jnp.where(first, 0, 1), turned(jnp.where(first, u, u - t - 1), yl)

    sides = ((kv_ref, 1 - c if last else c),)
    for u in range(units):
        q_yl, tt = unit(u)
        best = tops[q_yl]
        for i, (ref, core) in enumerate(sides):
            s = nt_dot(query[q_yl], ref[tt, :, :HD]) * SCALE
            if u == N_TP:
                s = s + hide(1, core)
            else:
                s = s + hide(0, core) * jnp.where(u == t, 1.0, 0.0)
            scores[u, i] = s
            best = jnp.maximum(best, jnp.maximum(s[:, :HD], s[:, HD:]))
        tops[q_yl] = best
    for b in range(2):
        tops[b] = jnp.broadcast_to(jnp.max(tops[b], axis=-1, keepdims=True), (size, HD))
        if last:
            scale = jnp.exp2(top_in[b] - tops[b])
            norms[b] = norm_in[b] * scale
            accs[b] = acc_in[b] * scale
        else:
            norms[b] = jnp.zeros((size, HD), jnp.float32)
            accs[b] = jnp.zeros((size, HD), jnp.float32)
    for u in range(units):
        q_yl, tt = unit(u)
        top = tops[q_yl]
        top = jnp.concatenate([top, top], axis=1)
        norm, acc = norms[q_yl], accs[q_yl]
        for i, (ref, _) in enumerate(sides):
            e = jnp.exp2(scores[u, i] - top)
            norm = norm + (e[:, :HD] + e[:, HD:])
            acc = acc + jnp.dot(
                e.astype(jnp.bfloat16), ref[tt, :, HD:], preferred_element_type=jnp.float32
            )
        norms[q_yl] = norm
        accs[q_yl] = acc
    if not last:
        return
    for b in range(2):
        rows = slice(b * P_DEV, (b + 1) * P_DEV)
        for q_yl in range(2):
            slot = 2 * b + q_yl
            total = jnp.sum(norms[q_yl, rows, :], axis=-1, keepdims=True)
            out_ref[slot, :P_DEV, :] = (accs[q_yl, rows, :] / total).astype(jnp.bfloat16)
            rest = as_row(tops[q_yl, rows, :1] + jnp.log2(total))
            pieces = []
            for _ in range(3):
                pieces.append(rest.astype(jnp.bfloat16).astype(jnp.float32))
                rest = rest - pieces[-1]
            pieces.append(jnp.zeros((13, HD), jnp.float32))
            out_ref[slot, P_DEV:, :] = jnp.concatenate(pieces, axis=0).astype(jnp.bfloat16)


def join_kernel(part_ref, out_ref):
    for a in range(2):
        parts, logs = [], []
        for i in (2 * a, 2 * a + 1):
            parts.append(part_ref[i, :P_DEV, :].astype(jnp.float32))
            tail = part_ref[i, P_DEV:, :].astype(jnp.float32)
            logs.append(as_column(tail[0:1, :] + tail[1:2, :] + tail[2:3, :]))
        top = jnp.maximum(*logs)
        scale = [jnp.exp2(log - top) for log in logs]
        mixed = (parts[0] * scale[0] + parts[1] * scale[1]) / (scale[0] + scale[1])
        out_ref[:, a * HD : (a + 1) * HD] = mixed.astype(jnp.bfloat16)


def call(body, outs, scratch, flops, *args, limit=VMEM):
    vmem = pl.BlockSpec(memory_space=pltpu.VMEM)
    return pl.pallas_call(
        body,
        out_shape=[jax.ShapeDtypeStruct(shape, dtype) for shape, dtype in outs],
        in_specs=[vmem] * len(args),
        out_specs=[vmem] * len(outs),
        scratch_shapes=[pltpu.VMEM(shape, dtype) for shape, dtype in scratch],
        compiler_params=pltpu.CompilerParams(vmem_limit_bytes=limit),
        cost_estimate=pl.CostEstimate(flops=flops, bytes_accessed=4 << 20, transcendentals=1 << 20),
    )(*args)


BF, F32 = jnp.bfloat16, jnp.float32


def run_start(*args):
    outs = [((N_TP, VALUES, 6 * HD), BF), ((2, MSG, HD), BF)]
    return call(start_kernel, outs, [], 1 << 28, *args, limit=56 << 20)


def run_encode(*args):
    outs = [((2 * P_DEV, HD), BF), ((N_TP, 2 * P_DEV, 2 * HD), BF)]
    scratch = [((N_TP, 256, 256), BF), ((N_TP, 256, 3 * HD), BF)]
    return call(encode_kernel, outs, scratch, 1 << 30, *args)


def run_latent(*args):
    return call(latent_kernel, [((P_DEV, 256), BF)], [], 1 << 26, *args)[0]


def run_attend(last, *args):
    size = 2 * P_DEV
    block = (2, size, HD)
    held = [((N_TP + 1, 1, size, size), F32), (block, BF)]
    state = [(block, F32)] * 3
    body = functools.partial(attend_kernel, last)
    if last:
        return call(body, [((4, PART, HD), BF)], held + state, 1 << 29, *args)[0]
    return call(body, state, held, 1 << 29, *args)


def run_join(*args):
    return call(join_kernel, [((P_DEV, 2 * HD), BF)], [], 1 << 20, *args)[0]


def on_device(
    byte_ids,
    patch_lens,
    byte_table,
    wq_cross,
    wk_cross,
    wv_cross,
    norm_gain,
    wq_latent,
    wk_latent,
    wv_latent,
):
    swap = [(0, 1), (1, 0)]
    turn = turns()

    tables, message = run_start(
        byte_ids.reshape(4, HD),
        patch_lens.reshape(1, HD),
        byte_table,
        wq_cross,
        wk_cross,
        wv_cross,
        wq_latent,
        wk_latent,
        wv_latent,
    )
    message = lax.ppermute(message, TURN, turn)
    tab_own = lax.all_to_all(tables, TP, 0, 0)
    byte_tables = (tab_own, lax.ppermute(tab_own, "c", swap))
    message = jnp.broadcast_to(message[:, None], (2, 16, MSG, HD)).reshape(32, MSG, HD)
    msg_own = lax.all_to_all(message, PLANES, 0, 0, tiled=True)
    msg_other = lax.ppermute(msg_own, "c", swap)

    q, kv = run_encode(*byte_tables, msg_own, msg_other, norm_gain.reshape(1, 2048))
    q_other = lax.ppermute(q, "yl", swap)
    kv_own = lax.all_to_all(kv, TP, 0, 0)
    patch_latent = run_latent(*byte_tables, msg_own, msg_other)
    kv_own, q_other, patch_latent = lax.optimization_barrier((kv_own, q_other, patch_latent))
    kv_other = lax.ppermute(kv_own, "c", swap)
    state = run_attend(False, q, q_other, kv_own)
    parts = run_attend(True, q, q_other, kv_other, *state)
    mixed = run_join(lax.all_to_all(parts, PAIR, 0, 0))
    latent_mixed = lax.ppermute(mixed, TURN, [(target, source) for source, target in turn])
    return (patch_latent, latent_mixed)


def solution(mesh):
    fine = Mesh(mesh.devices.reshape(8, 2, 2, 2, 4, 2), (*CTX, *TP))
    return jax.shard_map(
        on_device,
        mesh=fine,
        in_specs=(
            P(CTX),
            P(CTX),
            P(),
            P(None, TP),
            P(None, TP),
            P(None, TP),
            P(),
            P(CTX, TP),
            P(CTX, TP),
            P(CTX, TP),
        ),
        out_specs=(P(CTX, TP), P(CTX, TP)),
        check_vma=False,
    )
```
